512 devices in a mesh: tf: 128 (over y_hi, x, z), inp: 4 (over y_lo, core).
Axes of the slice: x: 4, y: 8 (y_hi: 4, y_lo: 2; y = y_hi * 2 + y_lo), z: 8, core: 2. Of those that a mesh axis runs over, the one named last changes fastest.
Arguments:
- voltages: bfloat16 [384, 2048, 1024], P('tf', None, 'inp'), may hold values from -6 to 6
- channel_gain: float32 [128, 1024], P(None, 'inp'), may hold values from 0.5 to 1.5
Outputs:
- visibility: float32 [128, 1024, 1024], P('tf', 'inp')
The draws below stay inside these ranges and needn't reach their ends.
All inputs are finite; a program needn't handle non-finite values.
Results may differ from the reference program's by a relative error of at most 0.0042.
Values may be sent and summed in bfloat16 or wider, within the bound.
No kernel may reach another device: no remote copies, remote signals or barrier semaphores. Data moves between devices by JAX's collectives and lax.ppermute only.
A program may use at most 64 MiB of HBM per device.

```python
import math
import jax
import jax.numpy as jnp
from jax import lax

NFFT = 2048
NI = 1024
TAPS = 4
SPECTRA = 384
CHAN = 128


def block_scale(key, extent, shards, least, largest):
    level = 1.0
    for axis_at, parts in shards:
        steps = jax.random.uniform(jax.random.fold_in(jax.random.fold_in(key, 6), axis_at), (parts,), jnp.float32, least / len(shards), largest / len(shards))
        level = level * jnp.repeat(jnp.exp(steps), extent[axis_at] // parts).reshape((-1,) + (1,) * (len(extent) - 1 - axis_at))
    return level


def centred(own_key, shape, width, reach, split=(), kind=jnp.bfloat16):
    values = jax.random.normal(own_key, shape, jnp.float32) * width
    if len(split) > 0:
        values = block_scale(own_key, shape, split, -0.22, 0.18) * values
    return jnp.clip(values, min=-reach, max=reach).astype(kind)


def setup_inputs(seed: int = 0) -> dict:
    key_list = jax.random.split(jax.random.key(seed), 3)
    voltages = centred(key_list[0], (SPECTRA, NFFT, NI), 1.0, 6.0, ((0, 128), (2, 4)))
    channel_gain = jnp.clip(1.0 + 0.1 * jax.random.normal(key_list[1], (CHAN, NI), jnp.float32), 0.5, 1.5)
    return dict(voltages=voltages, channel_gain=channel_gain)


def build_table(frame_len, channels, taps):
    length = taps * frame_len
    sample = jnp.arange(length).astype(jnp.float32)
    window = jnp.sinc((sample - length / 2 + 0.5) / frame_len) * (0.5 - 0.5 * jnp.cos(2.0 * math.pi * (sample + 0.5) / length))
    first_channel = (frame_len // 2 - channels) // 2
    phase_index = jnp.arange(frame_len, dtype=jnp.int32)[:, None] * (first_channel + jnp.arange(channels, dtype=jnp.int32))[None, :] % frame_len
    phase_angle = phase_index.astype(jnp.float32) * (2.0 * math.pi / frame_len)
    basis_cols = jnp.concatenate([jnp.cos(phase_angle), -jnp.sin(phase_angle)], axis=1)
    weighted = window.reshape(taps, frame_len)[:, :, None] * basis_cols[None]
    return (weighted / jnp.sqrt(jnp.sum(window * window))).astype(jnp.bfloat16)

def reference(voltages, channel_gain):
    tap_table = build_table(NFFT, CHAN, TAPS).astype(jnp.float32)
    padded = jnp.concatenate([jnp.zeros((TAPS - 1, NFFT, NI), jnp.bfloat16), voltages], axis=0)

    def one_spectrum(index):
        frames = lax.dynamic_slice_in_dim(padded, index, TAPS, 0).astype(jnp.float32)
        summed = jnp.einsum('kna,knc->ca', frames, tap_table)
        return (summed.reshape(2, CHAN, NI) * channel_gain[None]).astype(jnp.bfloat16)
    spectra = lax.map(one_spectrum, jnp.arange(SPECTRA, dtype=jnp.int32))
    norm_scale = 1.0 / math.sqrt(SPECTRA)
    input_index = jnp.arange(NI, dtype=jnp.int32)
    upper_half = input_index[:, None] <= input_index[None, :]

    def one_channel(channel):
        channel_block = lax.dynamic_index_in_dim(spectra, channel, 2, keepdims=False)
        real_part = channel_block[:, 0]
        imag_part = channel_block[:, 1]
        real_sum = jnp.dot(real_part.T, real_part, preferred_element_type=jnp.float32) + jnp.dot(imag_part.T, imag_part, preferred_element_type=jnp.float32)
        imag_sum = jnp.dot(imag_part.T, real_part, preferred_element_type=jnp.float32) - jnp.dot(real_part.T, imag_part, preferred_element_type=jnp.float32)
        return jnp.where(upper_half, real_sum, imag_sum) * norm_scale
    return lax.map(one_channel, jnp.arange(CHAN, dtype=jnp.int32))
```

```python
import functools
import math

import jax
import jax.numpy as jnp
from jax import lax
from jax.experimental import pallas as pl
from jax.experimental.pallas import tpu as pltpu
from jax.sharding import PartitionSpec as P

TAPS = 4
LANES = 128


def tap_window(frame_len):
    length = TAPS * frame_len
    shape = (length // LANES, LANES)
    sample = (
        lax.broadcasted_iota(jnp.int32, shape, 0) * LANES
        + lax.broadcasted_iota(jnp.int32, shape, 1)
    ).astype(jnp.float32)
    angle = math.pi * ((sample - length / 2 + 0.5) / frame_len)
    window = jnp.sin(angle) / angle * (
        0.5 - 0.5 * jnp.cos(2.0 * math.pi * (sample + 0.5) / length)
    )
    return window / jnp.sqrt(jnp.sum(window * window))


def fill_table(window_ref, table_ref, frame_len, channels):
    window_ref[...] = tap_window(frame_len)
    first_channel = (frame_len // 2 - channels) // 2
    rows = frame_len // LANES
    step = 2.0 * math.pi / frame_len
    channel = first_channel + lax.broadcasted_iota(jnp.int32, (channels, LANES), 0)
    lane = lax.broadcasted_iota(jnp.int32, (channels, LANES), 1)
    low = (channel * lane % frame_len).astype(jnp.float32) * step
    cos_low, sin_low = jnp.cos(low), jnp.sin(low)
    few = lax.broadcasted_iota(jnp.int32, (rows, LANES), 0) + first_channel
    part = lax.broadcasted_iota(jnp.int32, (rows, LANES), 1)
    high = (few * part % rows).astype(jnp.float32) * (2.0 * math.pi / rows)
    cos_high, sin_high = jnp.cos(high), jnp.sin(high)
    repeats = channels // rows

    def spread(values, h):
        column = jnp.broadcast_to(values[:, h : h + 1], (rows, LANES))
        return jnp.broadcast_to(column[None], (repeats, rows, LANES)).reshape(channels, LANES)

    for h in range(rows):
        cos_h, sin_h = spread(cos_high, h), spread(sin_high, h)
        cos_all = cos_low * cos_h - sin_low * sin_h
        sin_all = -(sin_low * cos_h + cos_low * sin_h)
        for k in range(TAPS):
            weight = window_ref[k * rows + h : k * rows + h + 1, :]
            at = slice(h * LANES, (h + 1) * LANES)
            table_ref[k, :channels, at] = (cos_all * weight).astype(jnp.bfloat16)
            table_ref[k, channels:, at] = (sin_all * weight).astype(jnp.bfloat16)


def partial_kernel(volts, kept, ahead, back, frames, table, window, sems):
    count, frame_len, width = frames.shape
    copies = [pltpu.make_async_copy(volts.at[f], frames.at[f], sems.at[f]) for f in range(count)]
    for copy in copies:
        copy.start()
    fill_table(window, table, frame_len, table.shape[1] // 2)
    for copy in copies:
        copy.wait()

    def spectrum(s):
        total = None
        for f in range(count):
            k = f + TAPS - 1 - s
            if 0 <= k < TAPS:
                product = jnp.dot(table[k], frames[f], preferred_element_type=jnp.float32)
                total = product if total is None else total + product
        return total

    ahead[0] = spectrum(4)
    ahead[1] = spectrum(5)
    back[0] = spectrum(0)
    for at, s in enumerate((1, 2, 3)):
        kept[at] = spectrum(s)


def partial_spectra(voltages, channels):
    count, frame_len, width = voltages.shape
    out = lambda n: jax.ShapeDtypeStruct((n, 2 * channels, width), jnp.float32)
    return pl.pallas_call(
        partial_kernel,
        out_shape=(out(3), out(2), out(1)),
        in_specs=[pl.BlockSpec(memory_space=pl.ANY)],
        out_specs=[pl.BlockSpec(memory_space=pltpu.VMEM)] * 3,
        scratch_shapes=[
            pltpu.VMEM((count, frame_len, width), jnp.bfloat16),
            pltpu.VMEM((TAPS, 2 * channels, frame_len), jnp.bfloat16),
            pltpu.VMEM((TAPS * frame_len // LANES, LANES), jnp.float32),
            pltpu.SemaphoreType.DMA((count,)),
        ],
        compiler_params=pltpu.CompilerParams(vmem_limit_bytes=32 * 1024 * 1024),
        cost_estimate=pl.CostEstimate(
            flops=2 * 12 * 2 * channels * frame_len * width,
            bytes_accessed=voltages.size * 2 + 6 * 2 * channels * width * 4,
            transcendentals=0,
        ),
    )(voltages)


def visibility_kernel(norm_scale, place, own, side, far, far_side, out, turned):
    rows, width = own.shape
    mine = place[0]
    plain = own[...].astype(jnp.float32)
    even = lax.broadcasted_iota(jnp.int32, (rows, width), 0) % 2 == 0
    turned[0] = own[...]
    turned[1] = jnp.where(even, jnp.roll(plain, -1, 0), -jnp.roll(plain, 1, 0)).astype(jnp.bfloat16)
    contract = (((0,), (0,)), ((), ()))

    def product(left, right):
        return lax.dot_general(left, right, contract, preferred_element_type=jnp.float32)

    def place_block(other, value):
        out[0, :, pl.ds(pl.multiple_of(other * width, width), width)] = value * norm_scale

    upper = lax.broadcasted_iota(jnp.int32, (width, width), 0) <= lax.broadcasted_iota(
        jnp.int32, (width, width), 1
    )
    place_block(
        mine, jnp.where(upper, product(turned[0], own[...]), product(turned[1], own[...]))
    )
    for flip, block in ((1, side), (2, far), (3, far_side)):
        other = mine ^ flip
        place_block(other, product(turned[(other < mine).astype(jnp.int32)], block[...]))


def visibilities(place, blocks, norm_scale):
    rows, width = blocks[0].shape
    return pl.pallas_call(
        functools.partial(visibility_kernel, norm_scale),
        out_shape=jax.ShapeDtypeStruct((1, width, 4 * width), jnp.float32),
        in_specs=[pl.BlockSpec(memory_space=pltpu.SMEM)]
        + [pl.BlockSpec(memory_space=pltpu.VMEM)] * 4,
        out_specs=pl.BlockSpec(memory_space=pltpu.VMEM),
        scratch_shapes=[pltpu.VMEM((2, rows, width), jnp.bfloat16)],
        compiler_params=pltpu.CompilerParams(vmem_limit_bytes=32 * 1024 * 1024),
        cost_estimate=pl.CostEstimate(
            flops=2 * 5 * rows * width * width,
            bytes_accessed=4 * rows * width * 2 + 4 * width * width * 4,
            transcendentals=0,
        ),
    )(place, *blocks)


def shards(voltages, channel_gain):
    channels, width = channel_gain.shape
    groups = lax.axis_size("tf")
    own_group = lax.axis_index("tf")
    kept, ahead, back = partial_spectra(voltages, channels)
    from_before = lax.ppermute(ahead, "tf", [(i, i + 1) for i in range(groups - 1)])
    from_after = lax.ppermute(back, "tf", [(i, (i - 1) % groups) for i in range(groups)])
    third = jnp.where(own_group == groups - 1, 0.0, kept[2:]) + from_after
    summed = jnp.concatenate([kept[:2] + from_before, third], axis=0)
    spectra = (
        summed.reshape(3, 2, channels, width) * channel_gain[None, None]
    ).astype(jnp.bfloat16)
    spectra = spectra.transpose(2, 0, 1, 3)
    turned = lax.all_to_all(spectra, "tf", split_axis=0, concat_axis=0, tiled=True)
    own = turned.reshape(groups * 6, width)
    far = lax.ppermute(own, "inp", [(i, i ^ 2) for i in range(4)])
    side = lax.ppermute(own, "inp", [(i, i ^ 1) for i in range(4)])
    far_side = lax.ppermute(far, "inp", [(i, i ^ 1) for i in range(4)])
    place = lax.axis_index("inp").astype(jnp.int32).reshape(1)
    norm_scale = 1.0 / math.sqrt(3 * groups)
    return visibilities(place, (own, side, far, far_side), norm_scale)


def solution(mesh):
    placed = (P("tf", None, "inp"), P(None, "inp"))
    return jax.shard_map(
        shards, mesh=mesh, in_specs=placed, out_specs=P("tf", "inp", None), check_vma=False
    )
```

```python
import functools
import math

import jax
import jax.numpy as jnp
from jax import lax
from jax.experimental import pallas as pl
from jax.experimental.pallas import tpu as pltpu
from jax.sharding import PartitionSpec as P

TAPS = 4
LANES = 128


def tap_window(frame_len):
    length = TAPS * frame_len
    shape = (length // LANES, LANES)
    sample = (
        lax.broadcasted_iota(jnp.int32, shape, 0) * LANES
        + lax.broadcasted_iota(jnp.int32, shape, 1)
    ).astype(jnp.float32)
    angle = math.pi * ((sample - length / 2 + 0.5) / frame_len)
    window = jnp.sin(angle) / angle * (
        0.5 - 0.5 * jnp.cos(2.0 * math.pi * (sample + 0.5) / length)
    )
    return window / jnp.sqrt(jnp.sum(window * window))


def fill_table(window_ref, table_ref, frame_len, channels):
    window_ref[...] = tap_window(frame_len)
    first_channel = (frame_len // 2 - channels) // 2
    rows = frame_len // LANES
    shape = (channels, LANES)
    channel = first_channel + lax.broadcasted_iota(jnp.int32, shape, 0)
    lane = lax.broadcasted_iota(jnp.int32, shape, 1)
    low = (channel * lane % frame_len).astype(jnp.float32) * (2.0 * math.pi / frame_len)
    cos_low, sin_low = jnp.cos(low), jnp.sin(low)
    few = lax.broadcasted_iota(jnp.int32, (rows, LANES), 0) + first_channel
    part = lax.broadcasted_iota(jnp.int32, (rows, LANES), 1)
    high = (few * part % rows).astype(jnp.float32) * (2.0 * math.pi / rows)
    cos_high, sin_high = jnp.cos(high), jnp.sin(high)
    repeats = channels // rows

    def spread(values, h):
        column = jnp.broadcast_to(values[:, h : h + 1], (rows, LANES))
        return jnp.broadcast_to(column[None], (repeats, rows, LANES)).reshape(shape)

    for h in range(rows):
        cos_h, sin_h = spread(cos_high, h), spread(sin_high, h)
        cos_all = cos_low * cos_h - sin_low * sin_h
        sin_all = -(sin_low * cos_h + cos_low * sin_h)
        for k in range(TAPS):
            weight = window_ref[k * rows + h : k * rows + h + 1, :]
            at = slice(h * LANES, (h + 1) * LANES)
            table_ref[k, :channels, at] = (cos_all * weight).astype(jnp.bfloat16)
            table_ref[k, channels:, at] = (sin_all * weight).astype(jnp.bfloat16)


def partial_kernel(volts, chunks, frames, table, window, rows, sems):
    count, frame_len, width = frames.shape
    channels = table.shape[1] // 2
    halves = width // LANES
    touched = count + TAPS - 1
    copies = [pltpu.make_async_copy(volts.at[f], frames.at[f], sems.at[f]) for f in range(count)]
    for copy in copies:
        copy.start()
    fill_table(window, table, frame_len, channels)
    for copy in copies:
        copy.wait()
    for s in range(touched):
        total = None
        for f in range(count):
            k = f + TAPS - 1 - s
            if 0 <= k < TAPS:
                product = jnp.dot(table[k], frames[f], preferred_element_type=jnp.float32)
                total = product if total is None else total + product
        for p in range(2):
            for h in range(halves):
                at = ((s * 2 + p) * halves + h) * channels
                rows[at : at + channels, :] = total[
                    p * channels : (p + 1) * channels, h * LANES : (h + 1) * LANES
                ]
    size = touched * 2 * halves
    together = 2

    def turn(step, carry):
        pieces = [
            rows[pl.ds(j * channels + step * together + q, 8, stride=channels), :]
            for q in range(together)
            for j in range(0, size, 8)
        ]
        start = pl.multiple_of(step * (together * size), together * size)
        chunks[pl.ds(start, together * size), :] = jnp.concatenate(pieces, 0).astype(jnp.bfloat16)
        return carry

    lax.fori_loop(0, channels // together, turn, 0, unroll=8)


def partial_spectra(voltages, channels):
    count, frame_len, width = voltages.shape
    size = (count + TAPS - 1) * 2 * (width // LANES)
    return pl.pallas_call(
        partial_kernel,
        out_shape=jax.ShapeDtypeStruct((channels * size, LANES), jnp.bfloat16),
        in_specs=[pl.BlockSpec(memory_space=pl.ANY)],
        out_specs=pl.BlockSpec(memory_space=pltpu.VMEM),
        scratch_shapes=[
            pltpu.VMEM((count, frame_len, width), jnp.bfloat16),
            pltpu.VMEM((TAPS, 2 * channels, frame_len), jnp.bfloat16),
            pltpu.VMEM((TAPS * frame_len // LANES, LANES), jnp.float32),
            pltpu.VMEM((size * channels, LANES), jnp.float32),
            pltpu.SemaphoreType.DMA((count,)),
        ],
        compiler_params=pltpu.CompilerParams(vmem_limit_bytes=60 * 1024 * 1024),
        cost_estimate=pl.CostEstimate(
            flops=2 * 12 * 2 * channels * frame_len * width,
            bytes_accessed=voltages.size * 2 + channels * size * LANES * 2,
            transcendentals=0,
        ),
    )(voltages)


def finish_kernel(count, place, chunks, gain, spectra, wide):
    groups = spectra.shape[0] // (2 * count)
    halves = spectra.shape[1] // LANES
    size = chunks.shape[0] // groups
    begun = count * 2 * halves
    wide[:size, :] = jnp.zeros((size, LANES), jnp.float32)
    wide[size:, :] = chunks[...].astype(jnp.float32)
    scale = gain[pl.ds(place[0], 1), :]
    for sp in range(2 * count):
        for h in range(halves):
            r = sp * halves + h
            own = wide[pl.ds(size + r, groups, stride=size), :]
            before = wide[pl.ds(begun + r, groups, stride=size), :]
            lanes = slice(h * LANES, (h + 1) * LANES)
            spectra[sp * groups : (sp + 1) * groups, lanes] = (
                (own + before) * scale[:, lanes]
            ).astype(jnp.bfloat16)


def finished_spectra(place, chunks, channel_gain, count, groups):
    width = channel_gain.shape[1]
    return pl.pallas_call(
        functools.partial(finish_kernel, count),
        out_shape=jax.ShapeDtypeStruct((2 * count * groups, width), jnp.bfloat16),
        in_specs=[pl.BlockSpec(memory_space=pltpu.SMEM)]
        + [pl.BlockSpec(memory_space=pltpu.VMEM)] * 2,
        out_specs=pl.BlockSpec(memory_space=pltpu.VMEM),
        scratch_shapes=[
            pltpu.VMEM((chunks.shape[0] + chunks.shape[0] // groups, LANES), jnp.float32)
        ],
        compiler_params=pltpu.CompilerParams(vmem_limit_bytes=16 * 1024 * 1024),
    )(place, chunks, channel_gain)


def product(left, right):
    return jnp.dot(left, right, preferred_element_type=jnp.float32)


def near_kernel(groups, norm_scale, place, own, side, far, out, turned, block, sems):
    rows, width = own.shape
    mine = place[0]
    turned[0] = own[...].T
    for s in range(rows // (2 * groups)):
        real = slice(2 * s * groups, (2 * s + 1) * groups)
        imag = slice((2 * s + 1) * groups, (2 * s + 2) * groups)
        turned[1, :, real] = turned[0, :, imag]
        turned[1, :, imag] = -turned[0, :, real]
    copies = []

    def place_block(at, other, value):
        block[at] = value * norm_scale
        columns = pl.ds(pl.multiple_of(other * width, width), width)
        copies.append(pltpu.make_async_copy(block.at[at], out.at[0, :, columns], sems.at[at]))
        copies[-1].start()

    upper = lax.broadcasted_iota(jnp.int32, (width, width), 0) <= lax.broadcasted_iota(
        jnp.int32, (width, width), 1
    )
    place_block(
        0, mine, jnp.where(upper, product(turned[0], own[...]), product(turned[1], own[...]))
    )
    for at, flip, right in ((1, 1, side), (2, 2, far)):
        other = mine ^ flip
        part = (other < mine).astype(jnp.int32)
        place_block(at, other, product(turned[part], right[...]))
    for copy in copies:
        copy.wait()


def last_kernel(norm_scale, place, turned, far_side, begun, out, block, sem):
    width = far_side.shape[1]
    other = place[0] ^ 3
    part = (other < place[0]).astype(jnp.int32)
    block[...] = product(turned[part], far_side[...]) * norm_scale
    columns = pl.ds(pl.multiple_of(other * width, width), width)
    copy = pltpu.make_async_copy(block, out.at[0, :, columns], sem)
    copy.start()
    copy.wait()


def shards(voltages, channel_gain):
    count = voltages.shape[0]
    channels, width = channel_gain.shape
    groups = lax.axis_size("tf")
    norm_scale = 1.0 / math.sqrt(count * groups)
    group = lax.axis_index("tf").astype(jnp.int32).reshape(1)
    place = lax.axis_index("inp").astype(jnp.int32).reshape(1)
    chunks = partial_spectra(voltages, channels).reshape(channels, -1, LANES)
    turned = lax.all_to_all(chunks, "tf", split_axis=0, concat_axis=0, tiled=True)
    own = finished_spectra(group, turned.reshape(-1, LANES), channel_gain, count, groups)
    far = lax.ppermute(own, "inp", [(i, i ^ 2) for i in range(4)])
    side = lax.ppermute(own, "inp", [(i, i ^ 1) for i in range(4)])
    far_side = lax.ppermute(far, "inp", [(i, i ^ 1) for i in range(4)])
    in_smem = pl.BlockSpec(memory_space=pltpu.SMEM)
    in_vmem = pl.BlockSpec(memory_space=pltpu.VMEM)
    anywhere = pl.BlockSpec(memory_space=pl.ANY)
    shape = jax.ShapeDtypeStruct((1, width, 4 * width), jnp.float32)
    begun, left = pl.pallas_call(
        functools.partial(near_kernel, groups, norm_scale),
        out_shape=(shape, jax.ShapeDtypeStruct((2, width, own.shape[0]), jnp.bfloat16)),
        in_specs=[in_smem, in_vmem, in_vmem, in_vmem],
        out_specs=(anywhere, in_vmem),
        scratch_shapes=[
            pltpu.VMEM((3, width, width), jnp.float32),
            pltpu.SemaphoreType.DMA((3,)),
        ],
        compiler_params=pltpu.CompilerParams(vmem_limit_bytes=16 * 1024 * 1024),
        cost_estimate=pl.CostEstimate(
            flops=2 * 4 * own.size * width, bytes_accessed=6 * own.size, transcendentals=0
        ),
    )(place, own, side, far)
    return pl.pallas_call(
        functools.partial(last_kernel, norm_scale),
        out_shape=shape,
        in_specs=[in_smem, in_vmem, in_vmem, anywhere],
        out_specs=anywhere,
        scratch_shapes=[pltpu.VMEM((width, width), jnp.float32), pltpu.SemaphoreType.DMA],
        input_output_aliases={3: 0},
        compiler_params=pltpu.CompilerParams(vmem_limit_bytes=16 * 1024 * 1024),
        cost_estimate=pl.CostEstimate(
            flops=2 * own.size * width, bytes_accessed=2 * own.size, transcendentals=0
        ),
    )(place, left, far_side, begun)


def solution(mesh):
    placed = (P("tf", None, "inp"), P(None, "inp"))
    return jax.shard_map(
        shards, mesh=mesh, in_specs=placed, out_specs=P("tf", "inp", None), check_vma=False
    )
```

```python
import functools
import math

import jax
import jax.numpy as jnp
from jax import lax
from jax.experimental import pallas as pl
from jax.experimental.pallas import tpu as pltpu
from jax.sharding import PartitionSpec as P

TAPS = 4
LANES = 128


def sine_ratio_and_cosine(angle):
    square = angle * angle

    def series(start):
        total = None
        for n in range(start + 10, start - 1, -2):
            term = (-1.0) ** (n // 2) / math.factorial(n)
            total = term if total is None else total * square + term
        return total

    return series(1), series(2) * square + 1.0


def cosine_and_sine(turns):
    half = (turns - 0.5) * math.pi
    ratio, cosine = sine_ratio_and_cosine(half)
    sine = ratio * half
    return 2.0 * sine * sine - 1.0, -2.0 * sine * cosine


def tap_window(frame_len):
    length = TAPS * frame_len
    shape = (length // LANES, LANES)
    sample = (
        lax.broadcasted_iota(jnp.int32, shape, 0) * LANES
        + lax.broadcasted_iota(jnp.int32, shape, 1)
    ).astype(jnp.float32)
    w = (sample + (0.5 - length / 2)) * (math.pi / 4 / frame_len)
    ratio, cosine = sine_ratio_and_cosine(w)
    sine = ratio * w
    window = ratio * (1.0 - 2.0 * sine * sine) * (cosine * cosine * cosine)
    return window * lax.rsqrt(jnp.sum(window * window))


def fill_table(window_ref, table_ref, frame_len, channels):
    window_ref[...] = tap_window(frame_len)
    first_channel = (frame_len // 2 - channels) // 2
    rows = frame_len // LANES
    shape = (channels, LANES)

    def angles(count, step, start, scale, period):
        row = lax.broadcasted_iota(jnp.int32, (count, LANES), 0) * step + start
        lane = lax.broadcasted_iota(jnp.int32, (count, LANES), 1)
        return cosine_and_sine((row * lane * scale % period).astype(jnp.float32) * (1.0 / period))

    cos_i, sin_i = angles(channels // 8, 8, first_channel, 1, frame_len)
    cos_j, sin_j = angles(8, 1, 0, 1, frame_len)
    cos_i, sin_i = cos_i[:, None, :], sin_i[:, None, :]
    cos_j, sin_j = cos_j[None], sin_j[None]
    cos_low = (cos_i * cos_j - sin_i * sin_j).reshape(shape)
    minus_sin_low = -(sin_i * cos_j + cos_i * sin_j).reshape(shape)
    cos_high, sin_high = angles(rows, 1, first_channel, 1, rows)
    repeats = channels // rows

    def spread(values, h):
        column = jnp.broadcast_to(values[:, h : h + 1], (rows, LANES))
        return jnp.broadcast_to(column[None], (repeats, rows, LANES)).reshape(shape)

    for h in range(rows):
        cos_h, sin_h = spread(cos_high, h), spread(sin_high, h)
        cos_all = cos_low * cos_h + minus_sin_low * sin_h
        minus_sin_all = minus_sin_low * cos_h - cos_low * sin_h
        for k in range(TAPS):
            weight = window_ref[k * rows + h : k * rows + h + 1, :]
            at = slice(k * frame_len + h * LANES, k * frame_len + (h + 1) * LANES)
            table_ref[:channels, at] = (cos_all * weight).astype(jnp.bfloat16)
            table_ref[channels:, at] = (minus_sin_all * weight).astype(jnp.bfloat16)


def partial_kernel(volts, chunks, frames, table, window, rows, turned, sems, out_sems):
    count, frame_len, width = volts.shape
    channels = table.shape[0] // 2
    halves = width // LANES
    touched = count + TAPS - 1
    pitch = channels + 8
    copies = [
        pltpu.make_async_copy(
            volts.at[f], frames.at[f * frame_len : (f + 1) * frame_len], sems.at[f]
        )
        for f in range(count)
    ]

    def meet(first, last, s):
        tap = first + TAPS - 1 - s
        return jnp.dot(
            table[:, tap * frame_len : (tap + last - first) * frame_len],
            frames[first * frame_len : last * frame_len],
            preferred_element_type=jnp.float32,
        )

    def store(s, total, add):
        for p in range(2):
            for h in range(halves):
                at = ((s * 2 + p) * halves + h) * pitch
                value = total[p * channels : (p + 1) * channels, h * LANES : (h + 1) * LANES]
                if add:
                    value = value + rows[at : at + channels, :]
                rows[at : at + channels, :] = value

    for copy in copies:
        copy.start()
    fill_table(window, table, frame_len, channels)
    copies[0].wait()
    for s in range(TAPS):
        store(s, meet(0, 1, s), False)
    for copy in copies[1:]:
        copy.wait()
    for s in range(1, touched):
        store(s, meet(max(1, s + 1 - TAPS), min(count, s + 1), s), s < TAPS)

    size = touched * 2 * halves
    together = 2
    blocks = 4
    steps = channels // together // blocks

    def turn(step, carry):
        pieces = [
            rows[pl.ds(j * pitch + step * together + q, 8, stride=pitch), :]
            for q in range(together)
            for j in range(0, size, 8)
        ]
        start = pl.multiple_of(step * (together * size), together * size)
        turned[pl.ds(start, together * size), :] = jnp.concatenate(pieces, 0).astype(jnp.bfloat16)
        return carry

    out_copies = []
    for block in range(blocks):
        lax.fori_loop(block * steps, (block + 1) * steps, turn, 0, unroll=16)
        part = pl.ds(block * steps * together * size, steps * together * size)
        out_copies.append(
            pltpu.make_async_copy(turned.at[part], chunks.at[part], out_sems.at[block])
        )
        out_copies[-1].start()
    for copy in out_copies:
        copy.wait()


def partial_spectra(voltages, channels):
    count, frame_len, width = voltages.shape
    size = (count + TAPS - 1) * 2 * (width // LANES)
    return pl.pallas_call(
        partial_kernel,
        out_shape=jax.ShapeDtypeStruct((channels * size, LANES), jnp.bfloat16),
        in_specs=[pl.BlockSpec(memory_space=pl.ANY)],
        out_specs=pl.BlockSpec(memory_space=pl.ANY),
        scratch_shapes=[
            pltpu.VMEM((count * frame_len, width), jnp.bfloat16),
            pltpu.VMEM((2 * channels, TAPS * frame_len), jnp.bfloat16),
            pltpu.VMEM((TAPS * frame_len // LANES, LANES), jnp.float32),
            pltpu.VMEM(((size + 1) * (channels + 8), LANES), jnp.float32),
            pltpu.VMEM((channels * size, LANES), jnp.bfloat16),
            pltpu.SemaphoreType.DMA((count,)),
            pltpu.SemaphoreType.DMA((4,)),
        ],
        compiler_params=pltpu.CompilerParams(vmem_limit_bytes=60 * 1024 * 1024),
        cost_estimate=pl.CostEstimate(
            flops=2 * 12 * 2 * channels * frame_len * width,
            bytes_accessed=voltages.size * 2 + channels * size * LANES * 2,
            transcendentals=0,
        ),
    )(voltages)


def finish_kernel(count, place, chunks, gain, spectra, wide):
    groups = spectra.shape[0] // (2 * count)
    halves = spectra.shape[1] // LANES
    size = chunks.shape[0] // groups
    begun = count * 2 * halves
    wide[:size, :] = jnp.zeros((size, LANES), jnp.float32)
    wide[size : size + chunks.shape[0], :] = chunks[...].astype(jnp.float32)
    scale = gain[pl.ds(place[0], 1), :]
    for sp in range(2 * count):
        for h in range(halves):
            r = sp * halves + h
            own = wide[pl.ds(size + r, groups, stride=size), :]
            before = wide[pl.ds(begun + r, groups, stride=size), :]
            lanes = slice(h * LANES, (h + 1) * LANES)
            spectra[sp * groups : (sp + 1) * groups, lanes] = (
                (own + before) * scale[:, lanes]
            ).astype(jnp.bfloat16)


def finished_spectra(place, chunks, channel_gain, count, groups):
    width = channel_gain.shape[1]
    return pl.pallas_call(
        functools.partial(finish_kernel, count),
        out_shape=jax.ShapeDtypeStruct((2 * count * groups, width), jnp.bfloat16),
        in_specs=[pl.BlockSpec(memory_space=pltpu.SMEM)]
        + [pl.BlockSpec(memory_space=pltpu.VMEM)] * 2,
        out_specs=pl.BlockSpec(memory_space=pltpu.VMEM),
        scratch_shapes=[
            pltpu.VMEM((chunks.shape[0] // groups * (groups + 2), LANES), jnp.float32)
        ],
        compiler_params=pltpu.CompilerParams(vmem_limit_bytes=16 * 1024 * 1024),
    )(place, chunks, channel_gain)


def product(left, right):
    return jnp.dot(left, right, preferred_element_type=jnp.float32)


def near_kernel(groups, norm_scale, place, own, side, far, out, turned, block, sems):
    rows, width = own.shape
    mine = place[0]
    turned[0] = own[...].T
    for s in range(rows // (2 * groups)):
        real = slice(2 * s * groups, (2 * s + 1) * groups)
        imag = slice((2 * s + 1) * groups, (2 * s + 2) * groups)
        turned[1, :, real] = turned[0, :, imag]
        turned[1, :, imag] = -turned[0, :, real]
    copies = []

    def place_block(at, other, value):
        block[at] = value * norm_scale
        columns = pl.ds(pl.multiple_of(other * width, width), width)
        copies.append(pltpu.make_async_copy(block.at[at], out.at[0, :, columns], sems.at[at]))
        copies[-1].start()

    upper = lax.broadcasted_iota(jnp.int32, (width, width), 0) <= lax.broadcasted_iota(
        jnp.int32, (width, width), 1
    )
    place_block(
        0, mine, jnp.where(upper, product(turned[0], own[...]), product(turned[1], own[...]))
    )
    for at, flip, right in ((1, 1, side), (2, 2, far)):
        other = mine ^ flip
        part = (other < mine).astype(jnp.int32)
        place_block(at, other, product(turned[part], right[...]))
    for copy in copies:
        copy.wait()


def last_kernel(norm_scale, place, turned, far_side, begun, out, block, sem):
    width = far_side.shape[1]
    other = place[0] ^ 3
    part = (other < place[0]).astype(jnp.int32)
    block[...] = product(turned[part], far_side[...]) * norm_scale
    columns = pl.ds(pl.multiple_of(other * width, width), width)
    copy = pltpu.make_async_copy(block, out.at[0, :, columns], sem)
    copy.start()
    copy.wait()


def shards(voltages, channel_gain):
    count = voltages.shape[0]
    channels, width = channel_gain.shape
    groups = lax.axis_size("tf")
    norm_scale = 1.0 / math.sqrt(count * groups)
    group = lax.axis_index("tf").astype(jnp.int32).reshape(1)
    place = lax.axis_index("inp").astype(jnp.int32).reshape(1)
    chunks = partial_spectra(voltages, channels).reshape(channels, -1, LANES)
    turned = lax.all_to_all(chunks, "tf", split_axis=0, concat_axis=0, tiled=True)
    own = finished_spectra(group, turned.reshape(-1, LANES), channel_gain, count, groups)
    far = lax.ppermute(own, "inp", [(i, i ^ 2) for i in range(4)])
    side = lax.ppermute(own, "inp", [(i, i ^ 1) for i in range(4)])
    far_side = lax.ppermute(far, "inp", [(i, i ^ 1) for i in range(4)])
    in_smem = pl.BlockSpec(memory_space=pltpu.SMEM)
    in_vmem = pl.BlockSpec(memory_space=pltpu.VMEM)
    anywhere = pl.BlockSpec(memory_space=pl.ANY)
    shape = jax.ShapeDtypeStruct((1, width, 4 * width), jnp.float32)
    begun, left = pl.pallas_call(
        functools.partial(near_kernel, groups, norm_scale),
        out_shape=(shape, jax.ShapeDtypeStruct((2, width, own.shape[0]), jnp.bfloat16)),
        in_specs=[in_smem, in_vmem, in_vmem, in_vmem],
        out_specs=(anywhere, in_vmem),
        scratch_shapes=[
            pltpu.VMEM((3, width, width), jnp.float32),
            pltpu.SemaphoreType.DMA((3,)),
        ],
        compiler_params=pltpu.CompilerParams(vmem_limit_bytes=16 * 1024 * 1024),
        cost_estimate=pl.CostEstimate(
            flops=2 * 4 * own.size * width, bytes_accessed=6 * own.size, transcendentals=0
        ),
    )(place, own, side, far)
    return pl.pallas_call(
        functools.partial(last_kernel, norm_scale),
        out_shape=shape,
        in_specs=[in_smem, in_vmem, in_vmem, anywhere],
        out_specs=anywhere,
        scratch_shapes=[pltpu.VMEM((width, width), jnp.float32), pltpu.SemaphoreType.DMA],
        input_output_aliases={3: 0},
        compiler_params=pltpu.CompilerParams(vmem_limit_bytes=16 * 1024 * 1024),
        cost_estimate=pl.CostEstimate(
            flops=2 * own.size * width, bytes_accessed=2 * own.size, transcendentals=0
        ),
    )(place, left, far_side, begun)


def solution(mesh):
    placed = (P("tf", None, "inp"), P(None, "inp"))
    return jax.shard_map(
        shards, mesh=mesh, in_specs=placed, out_specs=P("tf", "inp", None), check_vma=False
    )
```

```python
import functools
import math

import jax
import jax.numpy as jnp
from jax import lax
from jax.experimental import pallas as pl
from jax.experimental.pallas import tpu as pltpu
from jax.sharding import PartitionSpec as P

TAPS = 4
LANES = 128
LONG = 4
DEEP = 8


def sine_ratio_and_cosine(angle):
    square = angle * angle

    def series(start):
        total = None
        for n in range(start + 10, start - 1, -2):
            term = (-1.0) ** (n // 2) / math.factorial(n)
            total = term if total is None else total * square + term
        return total

    return series(1), series(2) * square + 1.0


def cosine_and_sine(turns):
    half = (turns - 0.5) * math.pi
    ratio, cosine = sine_ratio_and_cosine(half)
    sine = ratio * half
    return 2.0 * sine * sine - 1.0, -2.0 * sine * cosine


def tap_window(frame_len):
    length = TAPS * frame_len
    shape = (length // LANES, LANES)
    sample = (
        lax.broadcasted_iota(jnp.int32, shape, 0) * LANES
        + lax.broadcasted_iota(jnp.int32, shape, 1)
    ).astype(jnp.float32)
    w = (sample + (0.5 - length / 2)) * (math.pi / 4 / frame_len)
    ratio, cosine = sine_ratio_and_cosine(w)
    sine = ratio * w
    window = ratio * (1.0 - 2.0 * sine * sine) * (cosine * cosine * cosine)
    return window * lax.rsqrt(jnp.sum(window * window))


def fill_table(window_ref, table_ref, frame_len, channels):
    window_ref[...] = tap_window(frame_len)
    first_channel = (frame_len // 2 - channels) // 2
    rows = frame_len // LANES
    shape = (channels, LANES)

    def angles(count, step, start, scale, period):
        row = lax.broadcasted_iota(jnp.int32, (count, LANES), 0) * step + start
        lane = lax.broadcasted_iota(jnp.int32, (count, LANES), 1)
        return cosine_and_sine((row * lane * scale % period).astype(jnp.float32) * (1.0 / period))

    cos_i, sin_i = angles(channels // 8, 8, first_channel, 1, frame_len)
    cos_j, sin_j = angles(8, 1, 0, 1, frame_len)
    cos_i, sin_i = cos_i[:, None, :], sin_i[:, None, :]
    cos_j, sin_j = cos_j[None], sin_j[None]
    cos_low = (cos_i * cos_j - sin_i * sin_j).reshape(shape)
    minus_sin_low = -(sin_i * cos_j + cos_i * sin_j).reshape(shape)
    cos_high, sin_high = angles(rows, 1, first_channel, 1, rows)
    repeats = channels // rows

    def spread(values, h):
        column = jnp.broadcast_to(values[:, h : h + 1], (rows, LANES))
        return jnp.broadcast_to(column[None], (repeats, rows, LANES)).reshape(shape)

    for h in range(rows):
        cos_h, sin_h = spread(cos_high, h), spread(sin_high, h)
        cos_all = cos_low * cos_h + minus_sin_low * sin_h
        minus_sin_all = minus_sin_low * cos_h - cos_low * sin_h
        for k in range(TAPS):
            weight = window_ref[k * rows + h : k * rows + h + 1, :]
            at = slice(k * frame_len + h * LANES, k * frame_len + (h + 1) * LANES)
            table_ref[:channels, at] = (cos_all * weight).astype(jnp.bfloat16)
            table_ref[channels:, at] = (minus_sin_all * weight).astype(jnp.bfloat16)


def partial_kernel(volts, chunks, frames, table, window, rows, turned, sems, out_sems):
    count, frame_len, width = volts.shape
    channels = table.shape[0] // 2
    halves = width // LANES
    touched = count + TAPS - 1
    pitch = channels + 8
    copies = [
        pltpu.make_async_copy(
            volts.at[f], frames.at[f * frame_len : (f + 1) * frame_len], sems.at[f]
        )
        for f in range(count)
    ]

    def meet(first, last, s):
        tap = first + TAPS - 1 - s
        return jnp.dot(
            table[:, tap * frame_len : (tap + last - first) * frame_len],
            frames[first * frame_len : last * frame_len],
            preferred_element_type=jnp.float32,
        )

    def store(s, total, add):
        for p in range(2):
            for h in range(halves):
                at = ((s * 2 + p) * halves + h) * pitch
                value = total[p * channels : (p + 1) * channels, h * LANES : (h + 1) * LANES]
                if add:
                    value = value + rows[at : at + channels, :]
                rows[at : at + channels, :] = value

    for copy in copies:
        copy.start()
    fill_table(window, table, frame_len, channels)
    copies[0].wait()
    for s in range(TAPS):
        store(s, meet(0, 1, s), False)
    for copy in copies[1:]:
        copy.wait()
    for s in range(1, touched):
        store(s, meet(max(1, s + 1 - TAPS), min(count, s + 1), s), s < TAPS)

    size = touched * 2 * halves
    together = 2
    blocks = 4
    steps = channels // together // blocks

    def turn(step, carry):
        first = step * together
        place = first // LONG
        channel = place // DEEP * (LONG * DEEP) + first % LONG * DEEP + place % DEEP
        pieces = [
            rows[pl.ds(j * pitch + channel + q * DEEP, 8, stride=pitch), :]
            for q in range(together)
            for j in range(0, size, 8)
        ]
        start = pl.multiple_of(step * (together * size), together * size)
        turned[pl.ds(start, together * size), :] = jnp.concatenate(pieces, 0).astype(jnp.bfloat16)
        return carry

    out_copies = []
    for block in range(blocks):
        lax.fori_loop(block * steps, (block + 1) * steps, turn, 0, unroll=16)
        part = pl.ds(block * steps * together * size, steps * together * size)
        out_copies.append(
            pltpu.make_async_copy(turned.at[part], chunks.at[part], out_sems.at[block])
        )
        out_copies[-1].start()
    for copy in out_copies:
        copy.wait()


def partial_spectra(voltages, channels):
    count, frame_len, width = voltages.shape
    size = (count + TAPS - 1) * 2 * (width // LANES)
    return pl.pallas_call(
        partial_kernel,
        out_shape=jax.ShapeDtypeStruct((channels * size, LANES), jnp.bfloat16),
        in_specs=[pl.BlockSpec(memory_space=pl.ANY)],
        out_specs=pl.BlockSpec(memory_space=pl.ANY),
        scratch_shapes=[
            pltpu.VMEM((count * frame_len, width), jnp.bfloat16),
            pltpu.VMEM((2 * channels, TAPS * frame_len), jnp.bfloat16),
            pltpu.VMEM((TAPS * frame_len // LANES, LANES), jnp.float32),
            pltpu.VMEM(((size + 1) * (channels + 8), LANES), jnp.float32),
            pltpu.VMEM((channels * size, LANES), jnp.bfloat16),
            pltpu.SemaphoreType.DMA((count,)),
            pltpu.SemaphoreType.DMA((4,)),
        ],
        compiler_params=pltpu.CompilerParams(vmem_limit_bytes=60 * 1024 * 1024),
        cost_estimate=pl.CostEstimate(
            flops=2 * 12 * 2 * channels * frame_len * width,
            bytes_accessed=voltages.size * 2 + channels * size * LANES * 2,
            transcendentals=0,
        ),
    )(voltages)


def gather_kernel(count, place, chunks, gain, pieces, wide, ends):
    halves = gain.shape[1] // LANES
    half = count * 2 * halves
    size = 2 * half
    block = LONG * size
    sources = chunks.shape[0] // block
    runs = sources // DEEP
    length = half * (sources + runs)
    pitch = block + 8
    wide[:pitch, :] = jnp.zeros((pitch, LANES), jnp.float32)
    for source in range(sources):
        at = (source + 1) * pitch
        wide[at : at + block, :] = chunks[source * block : (source + 1) * block, :].astype(jnp.float32)
    inner = lax.broadcasted_iota(jnp.int32, (sources, LANES), 0) % DEEP > 0
    odd = lax.broadcasted_iota(jnp.int32, (half, LANES), 0) % halves
    for x in range(LONG):
        scale = gain[pl.ds(place[0] + x * DEEP, 1), :]
        first = x * 2 * length
        for r in range(half):
            h = r % halves
            own = wide[pl.ds(pitch + x * size + r, sources, stride=pitch), :]
            before = wide[pl.ds(x * size + half + r, sources, stride=pitch), :]
            value = (own + jnp.where(inner, before, 0.0)) * scale[:, h * LANES : (h + 1) * LANES]
            for copy in range(2):
                at = first + copy * length + r * sources
                pieces[at : at + sources, :] = value.astype(jnp.bfloat16)
        scales = scale[:, :LANES]
        for h in range(1, halves):
            scales = jnp.where(odd == h, scale[:, h * LANES : (h + 1) * LANES], scales)
        for y in range(runs):
            at = (y * DEEP + DEEP) * pitch + x * size + half
            ends[y * half : (y + 1) * half, :] = wide[at : at + half, :] * scales
        for copy in range(2):
            at = first + copy * length + half * sources
            pieces[at : at + half * runs, :] = ends[...].astype(jnp.bfloat16)


def gathered_pieces(place, chunks, channel_gain, count):
    half = count * 2 * (channel_gain.shape[1] // LANES)
    block = LONG * 2 * half
    sources = chunks.shape[0] // block
    runs = sources // DEEP
    return pl.pallas_call(
        functools.partial(gather_kernel, count),
        out_shape=jax.ShapeDtypeStruct((2 * LONG * half * (sources + runs), LANES), jnp.bfloat16),
        in_specs=[pl.BlockSpec(memory_space=pltpu.SMEM)]
        + [pl.BlockSpec(memory_space=pltpu.VMEM)] * 2,
        out_specs=pl.BlockSpec(memory_space=pltpu.VMEM),
        scratch_shapes=[
            pltpu.VMEM(((block + 8) * (sources + 3), LANES), jnp.float32),
            pltpu.VMEM((half * runs, LANES), jnp.float32),
        ],
        compiler_params=pltpu.CompilerParams(vmem_limit_bytes=16 * 1024 * 1024),
    )(place, chunks, channel_gain)


def column_kernel(count, sources, pieces, column, carried):
    width = column.shape[1]
    halves = width // LANES
    half = count * 2 * halves
    runs = sources // DEEP
    length = half * (sources + runs)
    steps = LONG * sources
    first_of_run = lax.broadcasted_iota(jnp.int32, (LONG * runs, DEEP, LANES), 1) == 0
    for chip in range(2):
        carried[:half, :] = jnp.zeros((half, LANES), jnp.float32)
        for x in range(LONG):
            for y in range(runs):
                run = y * LONG + x + 1
                if run < LONG * runs:
                    at = (x * 2 + chip) * length + half * sources + y * half
                    to = (run % LONG * runs + run // LONG) * half
                    carried[to : to + half, :] = pieces[at : at + half, :].astype(jnp.float32)
        for r in range(half):
            sp, h = r // halves, r % halves
            own = jnp.concatenate(
                [
                    pieces[
                        (x * 2 + chip) * length + r * sources : (x * 2 + chip) * length
                        + (r + 1) * sources,
                        :,
                    ]
                    for x in range(LONG)
                ],
                0,
            ).astype(jnp.float32)
            begun = carried[pl.ds(r, LONG * runs, stride=half), :]
            begun = jnp.where(first_of_run, begun[:, None, :], 0.0).reshape(steps, LANES)
            at = (chip * count * 2 + sp) * steps
            column[at : at + steps, h * LANES : (h + 1) * LANES] = (own + begun).astype(
                jnp.bfloat16
            )


def both_columns(pieces, count, width, groups):
    half = count * 2 * (width // LANES)
    sources = groups // LONG
    return pl.pallas_call(
        functools.partial(column_kernel, count, sources),
        out_shape=jax.ShapeDtypeStruct((4 * count * groups, width), jnp.bfloat16),
        in_specs=[pl.BlockSpec(memory_space=pltpu.VMEM)],
        out_specs=pl.BlockSpec(memory_space=pltpu.VMEM),
        scratch_shapes=[pltpu.VMEM((half * (groups // DEEP + 1), LANES), jnp.float32)],
        compiler_params=pltpu.CompilerParams(vmem_limit_bytes=16 * 1024 * 1024),
    )(pieces)


def product(left, right):
    return jnp.dot(left, right, preferred_element_type=jnp.float32)


def place_blocks(width, parts, out, block, sems):
    copies = []
    for at, (other, value) in enumerate(parts):
        block[at] = value
        columns = pl.ds(pl.multiple_of(other * width, width), width)
        copies.append(pltpu.make_async_copy(block.at[at], out.at[0, :, columns], sems.at[at]))
        copies[-1].start()
    for copy in copies:
        copy.wait()


def near_kernel(groups, norm_scale, place, column, out, turned, block, sems):
    rows, width = column.shape[0] // 2, column.shape[1]
    mine = place[0]
    chip = mine // 2
    own = column[pl.ds(pl.multiple_of(chip * rows, rows), rows), :]
    far = column[pl.ds(pl.multiple_of((1 - chip) * rows, rows), rows), :]
    turned[0] = own.T
    for s in range(rows // (2 * groups)):
        real = slice(2 * s * groups, (2 * s + 1) * groups)
        imag = slice((2 * s + 1) * groups, (2 * s + 2) * groups)
        turned[1, :, real] = turned[0, :, imag]
        turned[1, :, imag] = -turned[0, :, real]
    upper = lax.broadcasted_iota(jnp.int32, (width, width), 0) <= lax.broadcasted_iota(
        jnp.int32, (width, width), 1
    )
    diagonal = jnp.where(upper, product(turned[0], own), product(turned[1], own))
    other = mine ^ 2
    beside = product(turned[(other < mine).astype(jnp.int32)], far)
    parts = [(mine, diagonal * norm_scale), (other, beside * norm_scale)]
    place_blocks(width, parts, out, block, sems)


def last_kernel(norm_scale, place, turned, column, begun, out, block, sems):
    rows, width = column.shape[0] // 2, column.shape[1]
    mine = place[0]
    parts = []
    for chip in range(2):
        other = (mine ^ 1) % 2 + 2 * chip
        left = turned[(other < mine).astype(jnp.int32)]
        parts.append((other, product(left, column[chip * rows : (chip + 1) * rows]) * norm_scale))
    place_blocks(width, parts, out, block, sems)


def shards(voltages, channel_gain):
    count = voltages.shape[0]
    channels, width = channel_gain.shape
    groups = lax.axis_size("tf")
    norm_scale = 1.0 / math.sqrt(count * groups)
    group = lax.axis_index("tf").astype(jnp.int32)
    plane = LONG * DEEP
    base = (group // plane * plane + group % DEEP).reshape(1)
    place = lax.axis_index("inp").astype(jnp.int32).reshape(1)
    chunks = partial_spectra(voltages, channels).reshape(groups // LONG, -1, LANES)
    wheres = range(groups // plane)
    same_x = [
        [y * plane + x * DEEP + z for y in wheres for z in range(DEEP)] for x in range(LONG)
    ]
    turned = lax.all_to_all(
        chunks, "tf", split_axis=0, concat_axis=0, tiled=True, axis_index_groups=same_x
    )
    pieces = gathered_pieces(base, turned.reshape(-1, LANES), channel_gain, count)
    same_yz = [
        [(y * plane + x * DEEP + z) * 4 + chip * 2 + core for x in range(LONG) for chip in range(2)]
        for y in wheres
        for z in range(DEEP)
        for core in range(2)
    ]
    spread = lax.all_to_all(
        pieces.reshape(2 * LONG, -1, LANES),
        ("tf", "inp"),
        split_axis=0,
        concat_axis=0,
        tiled=True,
        axis_index_groups=same_yz,
    )
    column = both_columns(spread.reshape(-1, LANES), count, width, groups)
    other_column = lax.ppermute(column, "inp", [(i, i ^ 1) for i in range(4)])
    rows = column.shape[0] // 2
    in_smem = pl.BlockSpec(memory_space=pltpu.SMEM)
    in_vmem = pl.BlockSpec(memory_space=pltpu.VMEM)
    anywhere = pl.BlockSpec(memory_space=pl.ANY)
    shape = jax.ShapeDtypeStruct((1, width, 4 * width), jnp.float32)
    scratch = [pltpu.VMEM((2, width, width), jnp.float32), pltpu.SemaphoreType.DMA((2,))]
    limits = pltpu.CompilerParams(vmem_limit_bytes=16 * 1024 * 1024)
    cost = pl.CostEstimate(
        flops=6 * rows * width * width, bytes_accessed=8 * rows * width, transcendentals=0
    )
    begun, left = pl.pallas_call(
        functools.partial(near_kernel, groups, norm_scale),
        out_shape=(shape, jax.ShapeDtypeStruct((2, width, rows), jnp.bfloat16)),
        in_specs=[in_smem, in_vmem],
        out_specs=(anywhere, in_vmem),
        scratch_shapes=scratch,
        compiler_params=limits,
        cost_estimate=cost,
    )(place, column)
    return pl.pallas_call(
        functools.partial(last_kernel, norm_scale),
        out_shape=shape,
        in_specs=[in_smem, in_vmem, in_vmem, anywhere],
        out_specs=anywhere,
        scratch_shapes=scratch,
        input_output_aliases={3: 0},
        compiler_params=limits,
        cost_estimate=cost,
    )(place, left, other_column, begun)


def solution(mesh):
    placed = (P("tf", None, "inp"), P(None, "inp"))
    return jax.shard_map(
        shards, mesh=mesh, in_specs=placed, out_specs=P("tf", "inp", None), check_vma=False
    )
```

```python
import functools
import math

import jax
import jax.numpy as jnp
from jax import lax
from jax.experimental import pallas as pl
from jax.experimental.pallas import tpu as pltpu
from jax.sharding import PartitionSpec as P

TAPS = 4
LANES = 128
LONG = 4
DEEP = 8


def sine_ratio_and_cosine(angle):
    square = angle * angle

    def series(start):
        total = None
        for n in range(start + 10, start - 1, -2):
            term = (-1.0) ** (n // 2) / math.factorial(n)
            total = term if total is None else total * square + term
        return total

    return series(1), series(2) * square + 1.0


def cosine_and_sine(turns):
    half = (turns - 0.5) * math.pi
    ratio, cosine = sine_ratio_and_cosine(half)
    sine = ratio * half
    return 2.0 * sine * sine - 1.0, -2.0 * sine * cosine


def tap_window(frame_len):
    length = TAPS * frame_len
    shape = (length // LANES, LANES)
    sample = (
        lax.broadcasted_iota(jnp.int32, shape, 0) * LANES
        + lax.broadcasted_iota(jnp.int32, shape, 1)
    ).astype(jnp.float32)
    w = (sample + (0.5 - length / 2)) * (math.pi / 4 / frame_len)
    ratio, cosine = sine_ratio_and_cosine(w)
    sine = ratio * w
    window = ratio * (1.0 - 2.0 * sine * sine) * (cosine * cosine * cosine)
    return window * lax.rsqrt(jnp.sum(window * window))


def fill_table(window_ref, table_ref, frame_len, channels, halfway):
    window_ref[...] = tap_window(frame_len)
    first_channel = (frame_len // 2 - channels) // 2
    rows = frame_len // LANES
    shape = (channels, LANES)

    def angles(count, step, start, scale, period):
        row = lax.broadcasted_iota(jnp.int32, (count, LANES), 0) * step + start
        lane = lax.broadcasted_iota(jnp.int32, (count, LANES), 1)
        return cosine_and_sine((row * lane * scale % period).astype(jnp.float32) * (1.0 / period))

    cos_i, sin_i = angles(channels // 8, 8, first_channel, 1, frame_len)
    cos_j, sin_j = angles(8, 1, 0, 1, frame_len)
    cos_i, sin_i = cos_i[:, None, :], sin_i[:, None, :]
    cos_j, sin_j = cos_j[None], sin_j[None]
    cos_low = (cos_i * cos_j - sin_i * sin_j).reshape(shape)
    minus_sin_low = -(sin_i * cos_j + cos_i * sin_j).reshape(shape)
    cos_high, sin_high = angles(rows, 1, first_channel, 1, rows)
    repeats = channels // rows

    def spread(values, h):
        column = jnp.broadcast_to(values[:, h : h + 1], (rows, LANES))
        return jnp.broadcast_to(column[None], (repeats, rows, LANES)).reshape(shape)

    for h in range(rows):
        if h == rows // 2:
            halfway()
        cos_h, sin_h = spread(cos_high, h), spread(sin_high, h)
        cos_all = cos_low * cos_h + minus_sin_low * sin_h
        minus_sin_all = minus_sin_low * cos_h - cos_low * sin_h
        for k in range(TAPS):
            weight = window_ref[k * rows + h : k * rows + h + 1, :]
            at = slice(k * frame_len + h * LANES, k * frame_len + (h + 1) * LANES)
            table_ref[:channels, at] = (cos_all * weight).astype(jnp.bfloat16)
            table_ref[channels:, at] = (minus_sin_all * weight).astype(jnp.bfloat16)


def partial_kernel(volts, chunks, frames, table, window, rows, turned, sems, out_sems):
    count, frame_len, width = volts.shape
    channels = table.shape[0] // 2
    halves = width // LANES
    touched = count + TAPS - 1
    pitch = channels + 8
    copies = [
        pltpu.make_async_copy(
            volts.at[f], frames.at[f * frame_len : (f + 1) * frame_len], sems.at[f]
        )
        for f in range(count)
    ]

    def meet(first, last, s):
        tap = first + TAPS - 1 - s
        return jnp.dot(
            table[:, tap * frame_len : (tap + last - first) * frame_len],
            frames[first * frame_len : last * frame_len],
            preferred_element_type=jnp.float32,
        )

    def store(s, total, add):
        for p in range(2):
            for h in range(halves):
                at = ((s * 2 + p) * halves + h) * pitch
                value = total[p * channels : (p + 1) * channels, h * LANES : (h + 1) * LANES]
                if add:
                    value = value + rows[at : at + channels, :]
                rows[at : at + channels, :] = value

    copies[0].start()
    copies[1].start()

    def halfway():
        copies[0].wait()
        copies[2].start()

    fill_table(window, table, frame_len, channels, halfway)
    for s in range(TAPS):
        store(s, meet(0, 1, s), False)
    for copy in copies[1:]:
        copy.wait()
    for s in range(1, touched):
        store(s, meet(max(1, s + 1 - TAPS), min(count, s + 1), s), s < TAPS)

    size = touched * 2 * halves
    together = 2
    blocks = 4
    steps = channels // together // blocks

    def turn(step, carry):
        first = step * together
        place = first // LONG
        channel = place // DEEP * (LONG * DEEP) + first % LONG * DEEP + place % DEEP
        pieces = [
            rows[pl.ds(j * pitch + channel + q * DEEP, 8, stride=pitch), :]
            for q in range(together)
            for j in range(0, size, 8)
        ]
        start = pl.multiple_of(step * (together * size), together * size)
        turned[pl.ds(start, together * size), :] = jnp.concatenate(pieces, 0).astype(jnp.bfloat16)
        return carry

    out_copies = []
    for block in range(blocks):
        lax.fori_loop(block * steps, (block + 1) * steps, turn, 0, unroll=16)
        part = pl.ds(block * steps * together * size, steps * together * size)
        out_copies.append(
            pltpu.make_async_copy(turned.at[part], chunks.at[part], out_sems.at[block])
        )
        out_copies[-1].start()
    for copy in out_copies:
        copy.wait()


def partial_spectra(voltages, channels):
    count, frame_len, width = voltages.shape
    size = (count + TAPS - 1) * 2 * (width // LANES)
    return pl.pallas_call(
        partial_kernel,
        out_shape=jax.ShapeDtypeStruct((channels * size, LANES), jnp.bfloat16),
        in_specs=[pl.BlockSpec(memory_space=pl.ANY)],
        out_specs=pl.BlockSpec(memory_space=pl.ANY),
        scratch_shapes=[
            pltpu.VMEM((count * frame_len, width), jnp.bfloat16),
            pltpu.VMEM((2 * channels, TAPS * frame_len), jnp.bfloat16),
            pltpu.VMEM((TAPS * frame_len // LANES, LANES), jnp.float32),
            pltpu.VMEM(((size + 1) * (channels + 8), LANES), jnp.float32),
            pltpu.VMEM((channels * size, LANES), jnp.bfloat16),
            pltpu.SemaphoreType.DMA((count,)),
            pltpu.SemaphoreType.DMA((4,)),
        ],
        compiler_params=pltpu.CompilerParams(vmem_limit_bytes=60 * 1024 * 1024),
        cost_estimate=pl.CostEstimate(
            flops=2 * 12 * 2 * channels * frame_len * width,
            bytes_accessed=voltages.size * 2 + channels * size * LANES * 2,
            transcendentals=0,
        ),
    )(voltages)


def gather_kernel(count, place, chunks, gain, pieces, wide, ends):
    halves = gain.shape[1] // LANES
    half = count * 2 * halves
    size = 2 * half
    block = LONG * size
    sources = chunks.shape[0] // block
    runs = sources // DEEP
    length = half * (sources + runs)
    pitch = block + 8
    wide[:pitch, :] = jnp.zeros((pitch, LANES), jnp.float32)
    for source in range(sources):
        at = (source + 1) * pitch
        wide[at : at + block, :] = chunks[source * block : (source + 1) * block, :].astype(jnp.float32)
    inner = lax.broadcasted_iota(jnp.int32, (sources, LANES), 0) % DEEP > 0
    odd = lax.broadcasted_iota(jnp.int32, (half, LANES), 0) % halves
    for x in range(LONG):
        scale = gain[pl.ds(place[0] + x * DEEP, 1), :]
        first = x * 2 * length
        for r in range(half):
            h = r % halves
            own = wide[pl.ds(pitch + x * size + r, sources, stride=pitch), :]
            before = wide[pl.ds(x * size + half + r, sources, stride=pitch), :]
            value = (own + jnp.where(inner, before, 0.0)) * scale[:, h * LANES : (h + 1) * LANES]
            for copy in range(2):
                at = first + copy * length + r * sources
                pieces[at : at + sources, :] = value.astype(jnp.bfloat16)
        scales = scale[:, :LANES]
        for h in range(1, halves):
            scales = jnp.where(odd == h, scale[:, h * LANES : (h + 1) * LANES], scales)
        for y in range(runs):
            at = (y * DEEP + DEEP) * pitch + x * size + half
            ends[y * half : (y + 1) * half, :] = wide[at : at + half, :] * scales
        for copy in range(2):
            at = first + copy * length + half * sources
            pieces[at : at + half * runs, :] = ends[...].astype(jnp.bfloat16)


def gathered_pieces(place, chunks, channel_gain, count):
    half = count * 2 * (channel_gain.shape[1] // LANES)
    block = LONG * 2 * half
    sources = chunks.shape[0] // block
    runs = sources // DEEP
    return pl.pallas_call(
        functools.partial(gather_kernel, count),
        out_shape=jax.ShapeDtypeStruct((2 * LONG * half * (sources + runs), LANES), jnp.bfloat16),
        in_specs=[pl.BlockSpec(memory_space=pltpu.SMEM)]
        + [pl.BlockSpec(memory_space=pltpu.VMEM)] * 2,
        out_specs=pl.BlockSpec(memory_space=pltpu.VMEM),
        scratch_shapes=[
            pltpu.VMEM(((block + 8) * (sources + 3), LANES), jnp.float32),
            pltpu.VMEM((half * runs, LANES), jnp.float32),
        ],
        compiler_params=pltpu.CompilerParams(vmem_limit_bytes=16 * 1024 * 1024),
    )(place, chunks, channel_gain)


def column_kernel(count, sources, pieces, column, carried):
    width = column.shape[1]
    halves = width // LANES
    half = count * 2 * halves
    runs = sources // DEEP
    length = half * (sources + runs)
    steps = LONG * sources
    first_of_run = lax.broadcasted_iota(jnp.int32, (LONG * runs, DEEP, LANES), 1) == 0
    for chip in range(2):
        carried[:half, :] = jnp.zeros((half, LANES), jnp.float32)
        for x in range(LONG):
            at = (x * 2 + chip) * length + half * sources
            ends = pieces[at : at + half * runs, :].astype(jnp.float32)
            for y in range(runs):
                run = y * LONG + x + 1
                if run < LONG * runs:
                    to = (run % LONG * runs + run // LONG) * half
                    carried[to : to + half, :] = ends[y * half : (y + 1) * half]
        for r in range(half):
            sp, h = r // halves, r % halves
            own = jnp.concatenate(
                [
                    pieces[
                        (x * 2 + chip) * length + r * sources : (x * 2 + chip) * length
                        + (r + 1) * sources,
                        :,
                    ]
                    for x in range(LONG)
                ],
                0,
            ).astype(jnp.float32)
            begun = carried[pl.ds(r, LONG * runs, stride=half), :]
            begun = jnp.where(first_of_run, begun[:, None, :], 0.0).reshape(steps, LANES)
            at = (chip * count * 2 + sp) * steps
            column[at : at + steps, h * LANES : (h + 1) * LANES] = (own + begun).astype(
                jnp.bfloat16
            )


def both_columns(pieces, count, width, groups):
    half = count * 2 * (width // LANES)
    sources = groups // LONG
    return pl.pallas_call(
        functools.partial(column_kernel, count, sources),
        out_shape=jax.ShapeDtypeStruct((4 * count * groups, width), jnp.bfloat16),
        in_specs=[pl.BlockSpec(memory_space=pltpu.VMEM)],
        out_specs=pl.BlockSpec(memory_space=pltpu.VMEM),
        scratch_shapes=[pltpu.VMEM((half * (groups // DEEP + 1), LANES), jnp.float32)],
        compiler_params=pltpu.CompilerParams(vmem_limit_bytes=16 * 1024 * 1024),
    )(pieces)


def product(left, right):
    return jnp.dot(left, right, preferred_element_type=jnp.float32)


def place_blocks(width, parts, out, block, sems):
    copies = []
    for at, (other, value) in enumerate(parts):
        block[at] = value
        columns = pl.ds(pl.multiple_of(other * width, width), width)
        copies.append(pltpu.make_async_copy(block.at[at], out.at[0, :, columns], sems.at[at]))
        copies[-1].start()
    for copy in copies:
        copy.wait()


def near_kernel(groups, norm_scale, place, column, out, turned, block, sems):
    rows, width = column.shape[0] // 2, column.shape[1]
    mine = place[0]
    chip = mine // 2
    own = column[pl.ds(pl.multiple_of(chip * rows, rows), rows), :]
    far = column[pl.ds(pl.multiple_of((1 - chip) * rows, rows), rows), :]
    turned[0] = own.T
    for s in range(rows // (2 * groups)):
        real = slice(2 * s * groups, (2 * s + 1) * groups)
        imag = slice((2 * s + 1) * groups, (2 * s + 2) * groups)
        turned[1, :, real] = turned[0, :, imag]
        turned[1, :, imag] = -turned[0, :, real]
    upper = lax.broadcasted_iota(jnp.int32, (width, width), 0) <= lax.broadcasted_iota(
        jnp.int32, (width, width), 1
    )
    diagonal = jnp.where(upper, product(turned[0], own), product(turned[1], own))
    other = mine ^ 2
    beside = product(turned[(other < mine).astype(jnp.int32)], far)
    parts = [(mine, diagonal * norm_scale), (other, beside * norm_scale)]
    place_blocks(width, parts, out, block, sems)


def last_kernel(norm_scale, place, turned, column, begun, out, block, sems):
    rows, width = column.shape[0] // 2, column.shape[1]
    mine = place[0]
    parts = []
    for chip in range(2):
        other = (mine ^ 1) % 2 + 2 * chip
        left = turned[(other < mine).astype(jnp.int32)]
        parts.append((other, product(left, column[chip * rows : (chip + 1) * rows]) * norm_scale))
    place_blocks(width, parts, out, block, sems)


def shards(voltages, channel_gain):
    count = voltages.shape[0]
    channels, width = channel_gain.shape
    groups = lax.axis_size("tf")
    norm_scale = 1.0 / math.sqrt(count * groups)
    group = lax.axis_index("tf").astype(jnp.int32)
    plane = LONG * DEEP
    base = (group // plane * plane + group % DEEP).reshape(1)
    place = lax.axis_index("inp").astype(jnp.int32).reshape(1)
    chunks = partial_spectra(voltages, channels).reshape(groups // LONG, -1, LANES)
    wheres = range(groups // plane)
    same_x = [
        [y * plane + x * DEEP + z for y in wheres for z in range(DEEP)] for x in range(LONG)
    ]
    turned = lax.all_to_all(
        chunks, "tf", split_axis=0, concat_axis=0, tiled=True, axis_index_groups=same_x
    )
    pieces = gathered_pieces(base, turned.reshape(-1, LANES), channel_gain, count)
    same_yz = [
        [(y * plane + x * DEEP + z) * 4 + chip * 2 + core for x in range(LONG) for chip in range(2)]
        for y in wheres
        for z in range(DEEP)
        for core in range(2)
    ]
    spread = lax.all_to_all(
        pieces.reshape(2 * LONG, -1, LANES),
        ("tf", "inp"),
        split_axis=0,
        concat_axis=0,
        tiled=True,
        axis_index_groups=same_yz,
    )
    column = both_columns(spread.reshape(-1, LANES), count, width, groups)
    other_column = lax.ppermute(column, "inp", [(i, i ^ 1) for i in range(4)])
    rows = column.shape[0] // 2
    in_smem = pl.BlockSpec(memory_space=pltpu.SMEM)
    in_vmem = pl.BlockSpec(memory_space=pltpu.VMEM)
    anywhere = pl.BlockSpec(memory_space=pl.ANY)
    shape = jax.ShapeDtypeStruct((1, width, 4 * width), jnp.float32)
    scratch = [pltpu.VMEM((2, width, width), jnp.float32), pltpu.SemaphoreType.DMA((2,))]
    limits = pltpu.CompilerParams(vmem_limit_bytes=16 * 1024 * 1024)
    cost = pl.CostEstimate(
        flops=6 * rows * width * width, bytes_accessed=8 * rows * width, transcendentals=0
    )
    begun, left = pl.pallas_call(
        functools.partial(near_kernel, groups, norm_scale),
        out_shape=(shape, jax.ShapeDtypeStruct((2, width, rows), jnp.bfloat16)),
        in_specs=[in_smem, in_vmem],
        out_specs=(anywhere, in_vmem),
        scratch_shapes=scratch,
        compiler_params=limits,
        cost_estimate=cost,
    )(place, column)
    return pl.pallas_call(
        functools.partial(last_kernel, norm_scale),
        out_shape=shape,
        in_specs=[in_smem, in_vmem, in_vmem, anywhere],
        out_specs=anywhere,
        scratch_shapes=scratch,
        input_output_aliases={3: 0},
        compiler_params=limits,
        cost_estimate=cost,
    )(place, left, other_column, begun)


def solution(mesh):
    placed = (P("tf", None, "inp"), P(None, "inp"))
    return jax.shard_map(
        shards, mesh=mesh, in_specs=placed, out_specs=P("tf", "inp", None), check_vma=False
    )
```

```python
import functools
import math

import jax
import jax.numpy as jnp
from jax import lax
from jax.experimental import pallas as pl
from jax.experimental.pallas import tpu as pltpu
from jax.sharding import PartitionSpec as P

TAPS = 4
LANES = 128
LONG = 4
DEEP = 8


def sine_ratio_and_cosine(angle):
    square = angle * angle

    def series(start):
        total = None
        for n in range(start + 10, start - 1, -2):
            term = (-1.0) ** (n // 2) / math.factorial(n)
            total = term if total is None else total * square + term
        return total

    return series(1), series(2) * square + 1.0


def cosine_and_sine(turns):
    half = (turns - 0.5) * math.pi
    ratio, cosine = sine_ratio_and_cosine(half)
    sine = ratio * half
    return 2.0 * sine * sine - 1.0, -2.0 * sine * cosine


def tap_window(frame_len):
    length = TAPS * frame_len
    shape = (length // LANES, LANES)
    sample = (
        lax.broadcasted_iota(jnp.int32, shape, 0) * LANES
        + lax.broadcasted_iota(jnp.int32, shape, 1)
    ).astype(jnp.float32)
    w = (sample + (0.5 - length / 2)) * (math.pi / 4 / frame_len)
    ratio, cosine = sine_ratio_and_cosine(w)
    sine = ratio * w
    window = ratio * (1.0 - 2.0 * sine * sine) * (cosine * cosine * cosine)
    return window * lax.rsqrt(jnp.sum(window * window))


def fill_table(window_ref, table_ref, frame_len, channels, halfway):
    window_ref[...] = tap_window(frame_len)
    first_channel = (frame_len // 2 - channels) // 2
    rows = frame_len // LANES
    shape = (channels, LANES)

    def angles(count, step, start, scale, period):
        row = lax.broadcasted_iota(jnp.int32, (count, LANES), 0) * step + start
        lane = lax.broadcasted_iota(jnp.int32, (count, LANES), 1)
        return cosine_and_sine((row * lane * scale % period).astype(jnp.float32) * (1.0 / period))

    cos_i, sin_i = angles(channels // 8, 8, first_channel, 1, frame_len)
    cos_j, sin_j = angles(8, 1, 0, 1, frame_len)
    cos_i, sin_i = cos_i[:, None, :], sin_i[:, None, :]
    cos_j, sin_j = cos_j[None], sin_j[None]
    cos_low = (cos_i * cos_j - sin_i * sin_j).reshape(shape)
    minus_sin_low = -(sin_i * cos_j + cos_i * sin_j).reshape(shape)
    cos_high, sin_high = angles(rows, 1, first_channel, 1, rows)
    repeats = channels // rows

    def spread(values, h):
        column = jnp.broadcast_to(values[:, h : h + 1], (rows, LANES))
        return jnp.broadcast_to(column[None], (repeats, rows, LANES)).reshape(shape)

    for h in range(rows):
        if h == rows // 2:
            halfway()
        cos_h, sin_h = spread(cos_high, h), spread(sin_high, h)
        cos_all = cos_low * cos_h + minus_sin_low * sin_h
        minus_sin_all = minus_sin_low * cos_h - cos_low * sin_h
        for k in range(TAPS):
            weight = window_ref[k * rows + h : k * rows + h + 1, :]
            at = slice(k * frame_len + h * LANES, k * frame_len + (h + 1) * LANES)
            table_ref[:channels, at] = (cos_all * weight).astype(jnp.bfloat16)
            table_ref[channels:, at] = (minus_sin_all * weight).astype(jnp.bfloat16)


def partial_kernel(volts, chunks, frames, table, window, rows, turned, sems, out_sems):
    count, frame_len, width = volts.shape
    channels = table.shape[0] // 2
    halves = width // LANES
    touched = count + TAPS - 1
    pitch = channels + 8
    copies = [
        pltpu.make_async_copy(
            volts.at[f], frames.at[f * frame_len : (f + 1) * frame_len], sems.at[f]
        )
        for f in range(count)
    ]

    def meet(first, last, s):
        tap = first + TAPS - 1 - s
        return jnp.dot(
            table[:, tap * frame_len : (tap + last - first) * frame_len],
            frames[first * frame_len : last * frame_len],
            preferred_element_type=jnp.float32,
        )

    def store(s, total, add):
        for p in range(2):
            for h in range(halves):
                at = ((s * 2 + p) * halves + h) * pitch
                value = total[p * channels : (p + 1) * channels, h * LANES : (h + 1) * LANES]
                if add:
                    value = value + rows[at : at + channels, :]
                rows[at : at + channels, :] = value

    copies[0].start()
    copies[1].start()

    def halfway():
        copies[0].wait()
        copies[2].start()

    fill_table(window, table, frame_len, channels, halfway)
    for s in range(TAPS):
        store(s, meet(0, 1, s), False)
    for copy in copies[1:]:
        copy.wait()
    for s in range(1, touched):
        store(s, meet(max(1, s + 1 - TAPS), min(count, s + 1), s), s < TAPS)

    size = touched * 2 * halves
    together = 2
    blocks = 4
    steps = channels // together // blocks

    def turn(step, carry):
        first = step * together
        place = first // LONG
        channel = place // DEEP * (LONG * DEEP) + first % LONG * DEEP + place % DEEP
        pieces = [
            rows[pl.ds(j * pitch + channel + q * DEEP, 8, stride=pitch), :]
            for q in range(together)
            for j in range(0, size, 8)
        ]
        start = pl.multiple_of(step * (together * size), together * size)
        turned[pl.ds(start, together * size), :] = jnp.concatenate(pieces, 0).astype(jnp.bfloat16)
        return carry

    out_copies = []
    for block in range(blocks):
        lax.fori_loop(block * steps, (block + 1) * steps, turn, 0, unroll=16)
        part = pl.ds(block * steps * together * size, steps * together * size)
        out_copies.append(
            pltpu.make_async_copy(turned.at[part], chunks.at[part], out_sems.at[block])
        )
        out_copies[-1].start()
    for copy in out_copies:
        copy.wait()


def partial_spectra(voltages, channels):
    count, frame_len, width = voltages.shape
    size = (count + TAPS - 1) * 2 * (width // LANES)
    return pl.pallas_call(
        partial_kernel,
        out_shape=jax.ShapeDtypeStruct((channels * size, LANES), jnp.bfloat16),
        in_specs=[pl.BlockSpec(memory_space=pl.ANY)],
        out_specs=pl.BlockSpec(memory_space=pl.ANY),
        scratch_shapes=[
            pltpu.VMEM((count * frame_len, width), jnp.bfloat16),
            pltpu.VMEM((2 * channels, TAPS * frame_len), jnp.bfloat16),
            pltpu.VMEM((TAPS * frame_len // LANES, LANES), jnp.float32),
            pltpu.VMEM(((size + 1) * (channels + 8), LANES), jnp.float32),
            pltpu.VMEM((channels * size, LANES), jnp.bfloat16),
            pltpu.SemaphoreType.DMA((count,)),
            pltpu.SemaphoreType.DMA((4,)),
        ],
        compiler_params=pltpu.CompilerParams(vmem_limit_bytes=60 * 1024 * 1024),
        cost_estimate=pl.CostEstimate(
            flops=2 * 12 * 2 * channels * frame_len * width,
            bytes_accessed=voltages.size * 2 + channels * size * LANES * 2,
            transcendentals=0,
        ),
    )(voltages)


def gather_kernel(count, place, chunks, gain, pieces, wide, ends):
    halves = gain.shape[1] // LANES
    half = count * 2 * halves
    size = 2 * half
    block = LONG * size
    sources = chunks.shape[0] // block
    runs = sources // DEEP
    length = half * (sources + runs)
    pitch = block + 8
    wide[:pitch, :] = jnp.zeros((pitch, LANES), jnp.float32)
    for source in range(sources):
        at = (source + 1) * pitch
        wide[at : at + block, :] = chunks[source * block : (source + 1) * block, :].astype(jnp.float32)
    inner = lax.broadcasted_iota(jnp.int32, (sources, LANES), 0) % DEEP > 0
    odd = lax.broadcasted_iota(jnp.int32, (half, LANES), 0) % halves
    for x in range(LONG):
        scale = gain[pl.ds(place[0] + x * DEEP, 1), :]
        first = x * 2 * length
        for r in range(half):
            h = r % halves
            own = wide[pl.ds(pitch + x * size + r, sources, stride=pitch), :]
            before = wide[pl.ds(x * size + half + r, sources, stride=pitch), :]
            value = (own + jnp.where(inner, before, 0.0)) * scale[:, h * LANES : (h + 1) * LANES]
            for copy in range(2):
                at = first + copy * length + r * sources
                pieces[at : at + sources, :] = value.astype(jnp.bfloat16)
        scales = scale[:, :LANES]
        for h in range(1, halves):
            scales = jnp.where(odd == h, scale[:, h * LANES : (h + 1) * LANES], scales)
        for y in range(runs):
            at = (y * DEEP + DEEP) * pitch + x * size + half
            ends[y * half : (y + 1) * half, :] = wide[at : at + half, :] * scales
        for copy in range(2):
            at = first + copy * length + half * sources
            pieces[at : at + half * runs, :] = ends[...].astype(jnp.bfloat16)


def gathered_pieces(place, chunks, channel_gain, count):
    half = count * 2 * (channel_gain.shape[1] // LANES)
    block = LONG * 2 * half
    sources = chunks.shape[0] // block
    runs = sources // DEEP
    return pl.pallas_call(
        functools.partial(gather_kernel, count),
        out_shape=jax.ShapeDtypeStruct((2 * LONG * half * (sources + runs), LANES), jnp.bfloat16),
        in_specs=[pl.BlockSpec(memory_space=pltpu.SMEM)]
        + [pl.BlockSpec(memory_space=pltpu.VMEM)] * 2,
        out_specs=pl.BlockSpec(memory_space=pltpu.VMEM),
        scratch_shapes=[
            pltpu.VMEM(((block + 8) * (sources + 3), LANES), jnp.float32),
            pltpu.VMEM((half * runs, LANES), jnp.float32),
        ],
        compiler_params=pltpu.CompilerParams(vmem_limit_bytes=16 * 1024 * 1024),
    )(place, chunks, channel_gain)


def build_column(count, sources, pieces, column, carried, chip):
    width = column.shape[1]
    halves = width // LANES
    half = count * 2 * halves
    runs = sources // DEEP
    length = half * (sources + runs)
    steps = LONG * sources
    first_of_run = lax.broadcasted_iota(jnp.int32, (LONG * runs, DEEP, LANES), 1) == 0
    carried[:half, :] = jnp.zeros((half, LANES), jnp.float32)
    for x in range(LONG):
        at = (x * 2 + chip) * length + half * sources
        ends = pieces[at : at + half * runs, :].astype(jnp.float32)
        for y in range(runs):
            run = y * LONG + x + 1
            if run < LONG * runs:
                to = (run % LONG * runs + run // LONG) * half
                carried[to : to + half, :] = ends[y * half : (y + 1) * half]
    for r in range(half):
        sp, h = r // halves, r % halves
        own = jnp.concatenate(
            [
                pieces[
                    (x * 2 + chip) * length + r * sources : (x * 2 + chip) * length
                    + (r + 1) * sources,
                    :,
                ]
                for x in range(LONG)
            ],
            0,
        ).astype(jnp.float32)
        begun = carried[pl.ds(r, LONG * runs, stride=half), :]
        begun = jnp.where(first_of_run, begun[:, None, :], 0.0).reshape(steps, LANES)
        at = (chip * count * 2 + sp) * steps
        column[at : at + steps, h * LANES : (h + 1) * LANES] = (own + begun).astype(
            jnp.bfloat16
        )


def product(left, right):
    return jnp.dot(left, right, preferred_element_type=jnp.float32)


def place_blocks(width, parts, out, block, sems):
    copies = []
    for at, (other, value) in enumerate(parts):
        block[at] = value
        columns = pl.ds(pl.multiple_of(other * width, width), width)
        copies.append(pltpu.make_async_copy(block.at[at], out.at[0, :, columns], sems.at[at]))
        copies[-1].start()
    for copy in copies:
        copy.wait()


def near_kernel(count, groups, norm_scale, place, pieces, out, turned, column, carried, block, sems):
    rows, width = column.shape[0] // 2, column.shape[1]
    mine = place[0]
    chip = mine // 2
    for which in range(2):
        build_column(count, groups // LONG, pieces, column, carried, which)
    own = column[pl.ds(pl.multiple_of(chip * rows, rows), rows), :]
    far = column[pl.ds(pl.multiple_of((1 - chip) * rows, rows), rows), :]
    turned[0] = own.T
    for s in range(rows // (2 * groups)):
        real = slice(2 * s * groups, (2 * s + 1) * groups)
        imag = slice((2 * s + 1) * groups, (2 * s + 2) * groups)
        turned[1, :, real] = turned[0, :, imag]
        turned[1, :, imag] = -turned[0, :, real]
    upper = lax.broadcasted_iota(jnp.int32, (width, width), 0) <= lax.broadcasted_iota(
        jnp.int32, (width, width), 1
    )
    diagonal = jnp.where(upper, product(turned[0], own), product(turned[1], own))
    other = mine ^ 2
    beside = product(turned[(other < mine).astype(jnp.int32)], far)
    parts = [(mine, diagonal * norm_scale), (other, beside * norm_scale)]
    place_blocks(width, parts, out, block, sems)


def last_kernel(count, groups, norm_scale, place, turned, pieces, begun, out, column, carried, block, sems):
    rows, width = column.shape[0] // 2, column.shape[1]
    mine = place[0]
    copies = []
    for chip in range(2):
        build_column(count, groups // LONG, pieces, column, carried, chip)
        other = (mine ^ 1) % 2 + 2 * chip
        left = turned[(other < mine).astype(jnp.int32)]
        block[chip] = product(left, column[chip * rows : (chip + 1) * rows]) * norm_scale
        columns = pl.ds(pl.multiple_of(other * width, width), width)
        copies.append(pltpu.make_async_copy(block.at[chip], out.at[0, :, columns], sems.at[chip]))
        copies[-1].start()
    for copy in copies:
        copy.wait()


def shards(voltages, channel_gain):
    count = voltages.shape[0]
    channels, width = channel_gain.shape
    groups = lax.axis_size("tf")
    norm_scale = 1.0 / math.sqrt(count * groups)
    group = lax.axis_index("tf").astype(jnp.int32)
    plane = LONG * DEEP
    base = (group // plane * plane + group % DEEP).reshape(1)
    place = lax.axis_index("inp").astype(jnp.int32).reshape(1)
    chunks = partial_spectra(voltages, channels).reshape(groups // LONG, -1, LANES)
    wheres = range(groups // plane)
    same_x = [
        [y * plane + x * DEEP + z for y in wheres for z in range(DEEP)] for x in range(LONG)
    ]
    turned = lax.all_to_all(
        chunks, "tf", split_axis=0, concat_axis=0, tiled=True, axis_index_groups=same_x
    )
    pieces = gathered_pieces(base, turned.reshape(-1, LANES), channel_gain, count)
    same_yz = [
        [(y * plane + x * DEEP + z) * 4 + chip * 2 + core for x in range(LONG) for chip in range(2)]
        for y in wheres
        for z in range(DEEP)
        for core in range(2)
    ]
    spread = lax.all_to_all(
        pieces.reshape(2 * LONG, -1, LANES),
        ("tf", "inp"),
        split_axis=0,
        concat_axis=0,
        tiled=True,
        axis_index_groups=same_yz,
    )
    pieces = spread.reshape(-1, LANES)
    other_pieces = lax.ppermute(pieces, "inp", [(i, i ^ 1) for i in range(4)])
    rows = 2 * count * groups
    in_smem = pl.BlockSpec(memory_space=pltpu.SMEM)
    in_vmem = pl.BlockSpec(memory_space=pltpu.VMEM)
    anywhere = pl.BlockSpec(memory_space=pl.ANY)
    shape = jax.ShapeDtypeStruct((1, width, 4 * width), jnp.float32)
    half = count * 2 * (width // LANES)
    scratch = [
        pltpu.VMEM((2 * rows, width), jnp.bfloat16),
        pltpu.VMEM((half * (groups // DEEP + 1), LANES), jnp.float32),
        pltpu.VMEM((2, width, width), jnp.float32),
        pltpu.SemaphoreType.DMA((2,)),
    ]
    limits = pltpu.CompilerParams(vmem_limit_bytes=16 * 1024 * 1024)
    cost = pl.CostEstimate(
        flops=6 * rows * width * width, bytes_accessed=8 * rows * width, transcendentals=0
    )
    begun, left = pl.pallas_call(
        functools.partial(near_kernel, count, groups, norm_scale),
        out_shape=(shape, jax.ShapeDtypeStruct((2, width, rows), jnp.bfloat16)),
        in_specs=[in_smem, in_vmem],
        out_specs=(anywhere, in_vmem),
        scratch_shapes=scratch,
        compiler_params=limits,
        cost_estimate=cost,
    )(place, pieces)
    return pl.pallas_call(
        functools.partial(last_kernel, count, groups, norm_scale),
        out_shape=shape,
        in_specs=[in_smem, in_vmem, in_vmem, anywhere],
        out_specs=anywhere,
        scratch_shapes=scratch,
        input_output_aliases={3: 0},
        compiler_params=limits,
        cost_estimate=cost,
    )(place, left, other_pieces, begun)


def solution(mesh):
    placed = (P("tf", None, "inp"), P(None, "inp"))
    return jax.shard_map(
        shards, mesh=mesh, in_specs=placed, out_specs=P("tf", "inp", None), check_vma=False
    )
```

```python
import functools
import math

import jax
import jax.numpy as jnp
from jax import lax
from jax.experimental import pallas as pl
from jax.experimental.pallas import tpu as pltpu
from jax.sharding import PartitionSpec as P

TAPS = 4
LANES = 128
LONG = 4
DEEP = 8


def sine_ratio_and_cosine(angle):
    square = angle * angle

    def series(start):
        total = None
        for n in range(start + 10, start - 1, -2):
            term = (-1.0) ** (n // 2) / math.factorial(n)
            total = term if total is None else total * square + term
        return total

    return series(1), series(2) * square + 1.0


def cosine_and_sine(turns):
    half = (turns - 0.5) * math.pi
    ratio, cosine = sine_ratio_and_cosine(half)
    sine = ratio * half
    return 2.0 * sine * sine - 1.0, -2.0 * sine * cosine


def tap_window(frame_len):
    length = TAPS * frame_len
    shape = (length // LANES, LANES)
    sample = (
        lax.broadcasted_iota(jnp.int32, shape, 0) * LANES
        + lax.broadcasted_iota(jnp.int32, shape, 1)
    ).astype(jnp.float32)
    w = (sample + (0.5 - length / 2)) * (math.pi / 4 / frame_len)
    ratio, cosine = sine_ratio_and_cosine(w)
    sine = ratio * w
    window = ratio * (1.0 - 2.0 * sine * sine) * (cosine * cosine * cosine)
    return window * lax.rsqrt(jnp.sum(window * window))


def fill_table(window_ref, table_ref, frame_len, channels, halfway):
    window_ref[...] = tap_window(frame_len)
    first_channel = (frame_len // 2 - channels) // 2
    rows = frame_len // LANES
    shape = (channels, LANES)

    def angles(count, step, start, scale, period):
        row = lax.broadcasted_iota(jnp.int32, (count, LANES), 0) * step + start
        lane = lax.broadcasted_iota(jnp.int32, (count, LANES), 1)
        return cosine_and_sine((row * lane * scale % period).astype(jnp.float32) * (1.0 / period))

    cos_i, sin_i = angles(channels // 8, 8, first_channel, 1, frame_len)
    cos_j, sin_j = angles(8, 1, 0, 1, frame_len)
    cos_i, sin_i = cos_i[:, None, :], sin_i[:, None, :]
    cos_j, sin_j = cos_j[None], sin_j[None]
    cos_low = (cos_i * cos_j - sin_i * sin_j).reshape(shape)
    minus_sin_low = -(sin_i * cos_j + cos_i * sin_j).reshape(shape)
    cos_high, sin_high = angles(rows, 1, first_channel, 1, rows)
    repeats = channels // rows

    def spread(values, h):
        column = jnp.broadcast_to(values[:, h : h + 1], (rows, LANES))
        return jnp.broadcast_to(column[None], (repeats, rows, LANES)).reshape(shape)

    for h in range(rows):
        if h == rows // 2:
            halfway()
        cos_h, sin_h = spread(cos_high, h), spread(sin_high, h)
        cos_all = cos_low * cos_h + minus_sin_low * sin_h
        minus_sin_all = minus_sin_low * cos_h - cos_low * sin_h
        for k in range(TAPS):
            weight = window_ref[k * rows + h : k * rows + h + 1, :]
            at = slice(k * frame_len + h * LANES, k * frame_len + (h + 1) * LANES)
            table_ref[:channels, at] = (cos_all * weight).astype(jnp.bfloat16)
            table_ref[channels:, at] = (minus_sin_all * weight).astype(jnp.bfloat16)


def partial_kernel(volts, chunks, frames, table, window, rows, turned, sems, out_sems):
    count, frame_len, width = volts.shape
    channels = table.shape[0] // 2
    halves = width // LANES
    touched = count + TAPS - 1
    pitch = channels + 8
    copies = [
        pltpu.make_async_copy(
            volts.at[f], frames.at[f * frame_len : (f + 1) * frame_len], sems.at[f]
        )
        for f in range(count)
    ]

    def meet(first, last, s):
        tap = first + TAPS - 1 - s
        return jnp.dot(
            table[:, tap * frame_len : (tap + last - first) * frame_len],
            frames[first * frame_len : last * frame_len],
            preferred_element_type=jnp.float32,
        )

    def store(s, total, add):
        for p in range(2):
            for h in range(halves):
                at = ((s * 2 + p) * halves + h) * pitch
                value = total[p * channels : (p + 1) * channels, h * LANES : (h + 1) * LANES]
                if add:
                    value = value + rows[at : at + channels, :]
                rows[at : at + channels, :] = value

    copies[0].start()
    copies[1].start()

    def halfway():
        copies[0].wait()
        copies[2].start()

    fill_table(window, table, frame_len, channels, halfway)
    for s in range(TAPS):
        store(s, meet(0, 1, s), False)
    for copy in copies[1:]:
        copy.wait()
    for s in range(1, touched):
        store(s, meet(max(1, s + 1 - TAPS), min(count, s + 1), s), s < TAPS)

    size = touched * 2 * halves
    together = LONG
    blocks = 4
    steps = channels // together // blocks

    def turn(step, carry):
        first = step * together
        place = first // LONG
        channel = place // DEEP * (LONG * DEEP) + first % LONG * DEEP + place % DEEP
        pieces = [
            rows[pl.ds(j * pitch + channel + q * DEEP, 8, stride=pitch), :]
            for q in range(together)
            for j in range(0, size, 8)
        ]
        start = pl.multiple_of(step * (together * size), together * size)
        turned[pl.ds(start, together * size), :] = jnp.concatenate(pieces, 0).astype(jnp.bfloat16)
        return carry

    out_copies = []
    for block in range(blocks):
        lax.fori_loop(block * steps, (block + 1) * steps, turn, 0, unroll=8)
        part = pl.ds(block * steps * together * size, steps * together * size)
        out_copies.append(
            pltpu.make_async_copy(turned.at[part], chunks.at[part], out_sems.at[block])
        )
        out_copies[-1].start()
    for copy in out_copies:
        copy.wait()


def partial_spectra(voltages, channels):
    count, frame_len, width = voltages.shape
    size = (count + TAPS - 1) * 2 * (width // LANES)
    return pl.pallas_call(
        partial_kernel,
        out_shape=jax.ShapeDtypeStruct((channels * size, LANES), jnp.bfloat16),
        in_specs=[pl.BlockSpec(memory_space=pl.ANY)],
        out_specs=pl.BlockSpec(memory_space=pl.ANY),
        scratch_shapes=[
            pltpu.VMEM((count * frame_len, width), jnp.bfloat16),
            pltpu.VMEM((2 * channels, TAPS * frame_len), jnp.bfloat16),
            pltpu.VMEM((TAPS * frame_len // LANES, LANES), jnp.float32),
            pltpu.VMEM(((size + 1) * (channels + 8), LANES), jnp.float32),
            pltpu.VMEM((channels * size, LANES), jnp.bfloat16),
            pltpu.SemaphoreType.DMA((count,)),
            pltpu.SemaphoreType.DMA((4,)),
        ],
        compiler_params=pltpu.CompilerParams(vmem_limit_bytes=60 * 1024 * 1024),
        cost_estimate=pl.CostEstimate(
            flops=2 * 12 * 2 * channels * frame_len * width,
            bytes_accessed=voltages.size * 2 + channels * size * LANES * 2,
            transcendentals=0,
        ),
    )(voltages)


def gather_kernel(count, place, chunks, gain, pieces, wide, ends):
    halves = gain.shape[1] // LANES
    half = count * 2 * halves
    size = 2 * half
    block = LONG * size
    sources = chunks.shape[0] // block
    runs = sources // DEEP
    length = half * (sources + runs)
    pitch = block + 8
    wide[:pitch, :] = jnp.zeros((pitch, LANES), jnp.float32)
    for source in range(sources):
        at = (source + 1) * pitch
        wide[at : at + block, :] = chunks[source * block : (source + 1) * block, :].astype(jnp.float32)
    inner = lax.broadcasted_iota(jnp.int32, (sources, LANES), 0) % DEEP > 0
    odd = lax.broadcasted_iota(jnp.int32, (half, LANES), 0) % halves
    for x in range(LONG):
        scale = gain[pl.ds(place[0] + x * DEEP, 1), :]
        first = x * 2 * length
        for r in range(half):
            h = r % halves
            own = wide[pl.ds(pitch + x * size + r, sources, stride=pitch), :]
            before = wide[pl.ds(x * size + half + r, sources, stride=pitch), :]
            value = (own + jnp.where(inner, before, 0.0)) * scale[:, h * LANES : (h + 1) * LANES]
            for copy in range(2):
                at = first + copy * length + r * sources
                pieces[at : at + sources, :] = value.astype(jnp.bfloat16)
        scales = scale[:, :LANES]
        for h in range(1, halves):
            scales = jnp.where(odd == h, scale[:, h * LANES : (h + 1) * LANES], scales)
        for y in range(runs):
            at = (y * DEEP + DEEP) * pitch + x * size + half
            ends[y * half : (y + 1) * half, :] = wide[at : at + half, :] * scales
        for copy in range(2):
            at = first + copy * length + half * sources
            pieces[at : at + half * runs, :] = ends[...].astype(jnp.bfloat16)


def gathered_pieces(place, chunks, channel_gain, count):
    half = count * 2 * (channel_gain.shape[1] // LANES)
    block = LONG * 2 * half
    sources = chunks.shape[0] // block
    runs = sources // DEEP
    return pl.pallas_call(
        functools.partial(gather_kernel, count),
        out_shape=jax.ShapeDtypeStruct((2 * LONG * half * (sources + runs), LANES), jnp.bfloat16),
        in_specs=[pl.BlockSpec(memory_space=pltpu.SMEM)]
        + [pl.BlockSpec(memory_space=pltpu.VMEM)] * 2,
        out_specs=pl.BlockSpec(memory_space=pltpu.VMEM),
        scratch_shapes=[
            pltpu.VMEM(((block + 8) * (sources + 3), LANES), jnp.float32),
            pltpu.VMEM((half * runs, LANES), jnp.float32),
        ],
        compiler_params=pltpu.CompilerParams(vmem_limit_bytes=16 * 1024 * 1024),
    )(place, chunks, channel_gain)


def column_kernel(count, sources, pieces, column, carried):
    width = column.shape[1]
    halves = width // LANES
    half = count * 2 * halves
    runs = sources // DEEP
    length = half * (sources + runs)
    steps = LONG * sources
    first_of_run = lax.broadcasted_iota(jnp.int32, (LONG * runs, DEEP, LANES), 1) == 0
    for chip in range(2):
        carried[:half, :] = jnp.zeros((half, LANES), jnp.float32)
        for x in range(LONG):
            at = (x * 2 + chip) * length + half * sources
            ends = pieces[at : at + half * runs, :].astype(jnp.float32)
            for y in range(runs):
                run = y * LONG + x + 1
                if run < LONG * runs:
                    to = (run % LONG * runs + run // LONG) * half
                    carried[to : to + half, :] = ends[y * half : (y + 1) * half]
        for r in range(half):
            sp, h = r // halves, r % halves
            own = jnp.concatenate(
                [
                    pieces[
                        (x * 2 + chip) * length + r * sources : (x * 2 + chip) * length
                        + (r + 1) * sources,
                        :,
                    ]
                    for x in range(LONG)
                ],
                0,
            ).astype(jnp.float32)
            begun = carried[pl.ds(r, LONG * runs, stride=half), :]
            begun = jnp.where(first_of_run, begun[:, None, :], 0.0).reshape(steps, LANES)
            at = (chip * count * 2 + sp) * steps
            column[at : at + steps, h * LANES : (h + 1) * LANES] = (own + begun).astype(
                jnp.bfloat16
            )


def both_columns(pieces, count, width, groups):
    half = count * 2 * (width // LANES)
    sources = groups // LONG
    return pl.pallas_call(
        functools.partial(column_kernel, count, sources),
        out_shape=jax.ShapeDtypeStruct((4 * count * groups, width), jnp.bfloat16),
        in_specs=[pl.BlockSpec(memory_space=pltpu.VMEM)],
        out_specs=pl.BlockSpec(memory_space=pltpu.VMEM),
        scratch_shapes=[pltpu.VMEM((half * (groups // DEEP + 1), LANES), jnp.float32)],
        compiler_params=pltpu.CompilerParams(vmem_limit_bytes=16 * 1024 * 1024),
    )(pieces)


def product(left, right):
    return jnp.dot(left, right, preferred_element_type=jnp.float32)


def place_blocks(width, parts, out, block, sems):
    copies = []
    for at, (other, value) in enumerate(parts):
        block[at] = value
        columns = pl.ds(pl.multiple_of(other * width, width), width)
        copies.append(pltpu.make_async_copy(block.at[at], out.at[0, :, columns], sems.at[at]))
        copies[-1].start()
    for copy in copies:
        copy.wait()


def near_kernel(groups, norm_scale, place, column, out, turned, block, sems):
    rows, width = column.shape[0] // 2, column.shape[1]
    mine = place[0]
    chip = mine // 2
    own = column[pl.ds(pl.multiple_of(chip * rows, rows), rows), :]
    far = column[pl.ds(pl.multiple_of((1 - chip) * rows, rows), rows), :]
    turned[0] = own.T
    for s in range(rows // (2 * groups)):
        real = slice(2 * s * groups, (2 * s + 1) * groups)
        imag = slice((2 * s + 1) * groups, (2 * s + 2) * groups)
        turned[1, :, real] = turned[0, :, imag]
        turned[1, :, imag] = -turned[0, :, real]
    upper = lax.broadcasted_iota(jnp.int32, (width, width), 0) <= lax.broadcasted_iota(
        jnp.int32, (width, width), 1
    )
    diagonal = jnp.where(upper, product(turned[0], own), product(turned[1], own))
    other = mine ^ 2
    beside = product(turned[(other < mine).astype(jnp.int32)], far)
    parts = [(mine, diagonal * norm_scale), (other, beside * norm_scale)]
    place_blocks(width, parts, out, block, sems)


def last_kernel(norm_scale, place, turned, column, begun, out, block, sems):
    rows, width = column.shape[0] // 2, column.shape[1]
    mine = place[0]
    parts = []
    for chip in range(2):
        other = (mine ^ 1) % 2 + 2 * chip
        left = turned[(other < mine).astype(jnp.int32)]
        parts.append((other, product(left, column[chip * rows : (chip + 1) * rows]) * norm_scale))
    place_blocks(width, parts, out, block, sems)


def shards(voltages, channel_gain):
    count = voltages.shape[0]
    channels, width = channel_gain.shape
    groups = lax.axis_size("tf")
    norm_scale = 1.0 / math.sqrt(count * groups)
    group = lax.axis_index("tf").astype(jnp.int32)
    plane = LONG * DEEP
    base = (group // plane * plane + group % DEEP).reshape(1)
    place = lax.axis_index("inp").astype(jnp.int32).reshape(1)
    chunks = partial_spectra(voltages, channels).reshape(groups // LONG, -1, LANES)
    wheres = range(groups // plane)
    same_x = [
        [y * plane + x * DEEP + z for y in wheres for z in range(DEEP)] for x in range(LONG)
    ]
    turned = lax.all_to_all(
        chunks, "tf", split_axis=0, concat_axis=0, tiled=True, axis_index_groups=same_x
    )
    pieces = gathered_pieces(base, turned.reshape(-1, LANES), channel_gain, count)
    same_yz = [
        [(y * plane + x * DEEP + z) * 4 + chip * 2 + core for x in range(LONG) for chip in range(2)]
        for y in wheres
        for z in range(DEEP)
        for core in range(2)
    ]
    spread = lax.all_to_all(
        pieces.reshape(2 * LONG, -1, LANES),
        ("tf", "inp"),
        split_axis=0,
        concat_axis=0,
        tiled=True,
        axis_index_groups=same_yz,
    )
    column = both_columns(spread.reshape(-1, LANES), count, width, groups)
    other_column = lax.ppermute(column, "inp", [(i, i ^ 1) for i in range(4)])
    rows = column.shape[0] // 2
    in_smem = pl.BlockSpec(memory_space=pltpu.SMEM)
    in_vmem = pl.BlockSpec(memory_space=pltpu.VMEM)
    anywhere = pl.BlockSpec(memory_space=pl.ANY)
    shape = jax.ShapeDtypeStruct((1, width, 4 * width), jnp.float32)
    scratch = [pltpu.VMEM((2, width, width), jnp.float32), pltpu.SemaphoreType.DMA((2,))]
    limits = pltpu.CompilerParams(vmem_limit_bytes=16 * 1024 * 1024)
    cost = pl.CostEstimate(
        flops=6 * rows * width * width, bytes_accessed=8 * rows * width, transcendentals=0
    )
    begun, left = pl.pallas_call(
        functools.partial(near_kernel, groups, norm_scale),
        out_shape=(shape, jax.ShapeDtypeStruct((2, width, rows), jnp.bfloat16)),
        in_specs=[in_smem, in_vmem],
        out_specs=(anywhere, in_vmem),
        scratch_shapes=scratch,
        compiler_params=limits,
        cost_estimate=cost,
    )(place, column)
    return pl.pallas_call(
        functools.partial(last_kernel, norm_scale),
        out_shape=shape,
        in_specs=[in_smem, in_vmem, in_vmem, anywhere],
        out_specs=anywhere,
        scratch_shapes=scratch,
        input_output_aliases={3: 0},
        compiler_params=limits,
        cost_estimate=cost,
    )(place, left, other_column, begun)


def solution(mesh):
    placed = (P("tf", None, "inp"), P(None, "inp"))
    return jax.shard_map(
        shards, mesh=mesh, in_specs=placed, out_specs=P("tf", "inp", None), check_vma=False
    )
```
